512 devices in a mesh: own: 16 (over z, x_lo), fine: 32 (over y, x_hi, core).
Axes of the slice: x: 4 (x_hi: 2, x_lo: 2; x = x_hi * 2 + x_lo), y: 8, z: 8, core: 2. Of those that a mesh axis runs over, the one named last changes fastest.
Arguments:
- coarse_cells: bfloat16 [5, 256, 512, 128], P(None, 'own', 'fine'), may hold values from -6 to 6
- fine_cells: bfloat16 [2048, 5, 32, 1024], P(('own', 'fine')), may hold values from -6 to 6
- diffusivity: float32 [5], replicated, may hold values from 0.03 to 0.08
- patch_column: int32 [2048], P(('own', 'fine')), may hold values from 0 to 7, as said below
- patch_count: int32 [512], P(('own', 'fine')), may hold values from 0 to 4, as said below
- neighbor_slot: int32 [2048, 4], P(('own', 'fine')), may hold values from -1 to 3, as said below
Outputs:
- coarse_new: bfloat16 [5, 256, 512, 128], P(None, 'own', 'fine')
- fine_new: bfloat16 [2048, 5, 32, 1024], P(('own', 'fine'))
The draws below stay inside these ranges and needn't reach their ends.
Inputs may be any that keep to these rules, and one draw needn't show every extreme that they name: `patch_column`: on the devices of own index i, the 4 slots of a device hold, in some order, the 4 columns c of 0 to 7 whose pair c // 2 has the parity of i; only the first patch_count slots hold patches, so a footprint is never covered in two neighbouring slabs. `patch_count`: the counts of the devices of one own index sum to 4 * 32 // 2, and in every own index some device holds 4 patches. `neighbor_slot`: for the patch in slot s with column c on the device of fine index j: the slot of the patch at column c - 1 and c + 1 (modulo 8) on the same device, and of the patch at column c on fine index j - 1 and j + 1 (modulo the axis), or -1 where that footprint holds no patch; all four are -1 for slots that hold no patch.
All inputs are finite; a program needn't handle non-finite values.
Results may differ from the reference program's by a relative error of at most 0.0043.
Values may be sent and summed in bfloat16 or wider, within the bound.
No kernel may reach another device: no remote copies, remote signals or barrier semaphores. Data moves between devices by JAX's collectives and lax.ppermute only.
A program may use at most 128 MiB of HBM per device.

```python
import math
import jax
import jax.numpy as jnp
from jax import lax

NCOMP = 5
PATCH = 32
HALF = 16
FX = 8
PMAX = 4
SLOTS = 2048
NZ = 256
NY = 512
NX = 128
N_OWN = 16
N_FINE = 32


def patch_layout(key):
    slot_ids = jnp.arange(PMAX, dtype=jnp.int32)
    own_ids = jnp.arange(N_OWN, dtype=jnp.int32)
    eligible = 2 * (2 * (slot_ids[None, :] // 2) + own_ids[:, None] % 2) + slot_ids[None, :] % 2
    order_keys = jax.random.split(jax.random.fold_in(key, 11), N_OWN * N_FINE)
    orders = jax.vmap(lambda one_key: jax.random.permutation(one_key, PMAX))(order_keys)
    orders = orders.reshape(N_OWN, N_FINE, PMAX).astype(jnp.int32)
    columns = jnp.take_along_axis(jnp.broadcast_to(eligible[:, None, :], (N_OWN, N_FINE, PMAX)), orders, axis=2)
    pair_keys = jax.random.split(jax.random.fold_in(key, 12), N_OWN)
    dealt_order = jax.vmap(lambda one_key: jax.random.permutation(one_key, N_FINE))(pair_keys).astype(jnp.int32)
    shares = jax.random.randint(jax.random.fold_in(key, 13), (N_OWN, N_FINE // 2), 0, PMAX + 1, dtype=jnp.int32)
    shares = shares.at[:, 0].set(PMAX)
    values = jnp.stack([shares, PMAX - shares], axis=-1).reshape(N_OWN, N_FINE)
    counts = jnp.zeros((N_OWN, N_FINE), jnp.int32).at[own_ids[:, None], dealt_order].set(values)
    live_mask = slot_ids[None, None, :] < counts[:, :, None]
    column_ids = jnp.arange(FX, dtype=jnp.int32)
    holder = jnp.sum(jnp.where((columns[..., None] == column_ids) & live_mask[..., None], slot_ids[None, None, :, None] + 1, 0), axis=2) - 1
    left_slot = jnp.take_along_axis(holder, (columns - 1) % FX, axis=2)
    right_slot = jnp.take_along_axis(holder, (columns + 1) % FX, axis=2)
    below_slot = jnp.take_along_axis(jnp.roll(holder, 1, axis=1), columns, axis=2)
    above_slot = jnp.take_along_axis(jnp.roll(holder, -1, axis=1), columns, axis=2)
    neighbors = jnp.stack([left_slot, right_slot, below_slot, above_slot], axis=-1)
    neighbors = jnp.where(live_mask[..., None], neighbors, -1)
    return (columns.reshape(-1).astype(jnp.int32), counts.reshape(-1).astype(jnp.int32), neighbors.reshape(N_OWN * N_FINE * PMAX, 4).astype(jnp.int32))


def draw_patch_column(key, part):
    return patch_layout(key)[0]


def draw_patch_count(key, part):
    return patch_layout(key)[1]


def draw_neighbor_slot(key, part):
    return patch_layout(key)[2]


def levels(own_key, shape, cuts, least, high):
    factor_of = 1.0
    for dim, parts in cuts:
        heights = jax.random.uniform(jax.random.fold_in(jax.random.fold_in(own_key, 6), dim), (parts,), jnp.float32, least / len(cuts), high / len(cuts))
        factor_of = factor_of * jnp.repeat(jnp.exp(heights), shape[dim] // parts).reshape((-1,) + (1,) * (len(shape) - 1 - dim))
    return factor_of


def normal_values(stream_key, dims, deviation, most, cuts=(), kind=jnp.bfloat16):
    entries = deviation * jax.random.normal(stream_key, dims, jnp.float32)
    if cuts:
        entries = entries * levels(stream_key, dims, cuts, -0.22, 0.18)
    return jnp.clip(entries, -most, most).astype(kind)


def setup_inputs(seed: int = 0) -> dict:
    keys = jax.random.split(jax.random.key(seed), 7)
    coarse_cells = normal_values(keys[0], (NCOMP, NZ, NY, NX), 1.0, 6.0, ((1, 16), (2, 32)))
    fine_cells = normal_values(keys[1], (SLOTS, NCOMP, PATCH, PATCH * PATCH), 1.0, 6.0, ((0, 512),))
    diffusivity = jnp.clip(jnp.exp(jax.random.uniform(keys[2], (NCOMP,), jnp.float32, math.log(0.03), math.log(0.08))), 0.03, 0.08)
    patch_column = draw_patch_column(jax.random.fold_in(keys[6], 71), 0)
    patch_count = draw_patch_count(jax.random.fold_in(keys[6], 71), 0)
    neighbor_slot = draw_neighbor_slot(jax.random.fold_in(keys[6], 71), 0)
    return dict(coarse_cells=coarse_cells, fine_cells=fine_cells, diffusivity=diffusivity, patch_column=patch_column, patch_count=patch_count, neighbor_slot=neighbor_slot)


def spread(layer_in):
    return jnp.repeat(jnp.repeat(layer_in, 2, axis=-1), 2, axis=-2)


def pooled(layer_in):
    shape_in = layer_in.shape
    return layer_in.reshape(shape_in[:-2] + (shape_in[-2] // 2, 2, shape_in[-1] // 2, 2)).sum(axis=(-1, -3))


def fine_faces(blocked):
    return (blocked[..., 0], blocked[..., -1], blocked[..., 0, :], blocked[..., -1, :], blocked[:, :, 0], blocked[:, :, -1])


def box_faces(box_set, offset):
    low_at = offset
    high_at = box_set.shape[-1] - 1 - offset
    middle = slice(1, -1)
    return (box_set[:, :, middle, middle, low_at], box_set[:, :, middle, middle, high_at],
            box_set[:, :, middle, low_at, middle], box_set[:, :, middle, high_at, middle],
            box_set[:, :, low_at, middle, middle], box_set[:, :, high_at, middle, middle])


def periodic_change(values):
    summed = -6.0 * values
    for axis_id in (1, 2, 3):
        summed = summed + jnp.roll(values, 1, axis=axis_id) + jnp.roll(values, -1, axis=axis_id)
    return summed


def diffuse_cube(blocked, ghost_set):
    padded = jnp.pad(blocked, ((0, 0), (0, 0), (1, 1), (1, 1), (1, 1)))
    padded = padded.at[:, :, 1:-1, 1:-1, 0].set(ghost_set[0])
    padded = padded.at[:, :, 1:-1, 1:-1, -1].set(ghost_set[1])
    padded = padded.at[:, :, 1:-1, 0, 1:-1].set(ghost_set[2])
    padded = padded.at[:, :, 1:-1, -1, 1:-1].set(ghost_set[3])
    padded = padded.at[:, :, 0, 1:-1, 1:-1].set(ghost_set[4])
    padded = padded.at[:, :, -1, 1:-1, 1:-1].set(ghost_set[5])
    middle = padded[:, :, 1:-1, 1:-1, 1:-1]
    summed = padded[:, :, 1:-1, 1:-1, 2:] + padded[:, :, 1:-1, 1:-1, :-2]
    summed = summed + padded[:, :, 1:-1, 2:, 1:-1] + padded[:, :, 1:-1, :-2, 1:-1]
    summed = summed + padded[:, :, 2:, 1:-1, 1:-1] + padded[:, :, :-2, 1:-1, 1:-1]
    return summed - 6.0 * middle


def reference(coarse_cells, fine_cells, diffusivity, patch_column, patch_count, neighbor_slot):
    edge_len = PATCH
    half_len = HALF
    row_slots = N_FINE * PMAX
    coarse_rate = diffusivity[:, None, None, None]
    face_rate = diffusivity[:, None, None]
    old_level = coarse_cells.astype(jnp.float32)
    mid_level = old_level + coarse_rate * periodic_change(old_level)
    slab_fine = fine_cells.reshape(N_OWN, row_slots, NCOMP, edge_len, edge_len, edge_len)
    slab_columns = patch_column.reshape(N_OWN, row_slots)
    slab_counts = patch_count.reshape(N_OWN, N_FINE)
    slab_links = neighbor_slot.reshape(N_OWN, row_slots, 4)
    anchor = jnp.zeros((), jnp.int32)
    steps_h = jnp.arange(half_len, dtype=jnp.int32)
    strip_index = jnp.arange(row_slots, dtype=jnp.int32) // PMAX
    slot_index = jnp.arange(row_slots, dtype=jnp.int32) % PMAX
    shape_three = (row_slots, half_len, half_len)

    def place_slab(target, z_index, y_index, x_index, values):
        return target.at[:, jnp.broadcast_to(z_index, shape_three), jnp.broadcast_to(y_index, shape_three),
                         jnp.broadcast_to(x_index, shape_three)].add(jnp.transpose(values, (1, 0, 2, 3)))

    def place_plane(target, y_index, x_index, values):
        return target.at[:, jnp.broadcast_to(y_index, shape_three), jnp.broadcast_to(x_index, shape_three)].add(
            jnp.transpose(values, (1, 0, 2, 3)))

    def one_slab(item):
        own_index, patches, columns, counts, links = item
        planes = (own_index * half_len - 1 + jnp.arange(half_len + 2, dtype=jnp.int32)) % NZ
        wrap_pad = ((0, 0), (0, 0), (1, 1), (1, 1))
        old_block = jnp.pad(jnp.take(old_level, planes, axis=1), wrap_pad, mode="wrap")
        mid_block = jnp.pad(jnp.take(mid_level, planes, axis=1), wrap_pad, mode="wrap")
        y_start = strip_index * half_len
        x_start = columns.astype(jnp.int32) * half_len

        def cut_boxes(block):
            return jax.vmap(lambda row_at, col_at: lax.dynamic_slice(
                block, (anchor, anchor, row_at, col_at),
                (NCOMP, half_len + 2, half_len + 2, half_len + 2)))(y_start, x_start)

        old_boxes = cut_boxes(old_block)
        mid_boxes = cut_boxes(mid_block)
        old_ghost = box_faces(old_boxes, 0)
        old_inner = box_faces(old_boxes, 1)
        mid_ghost = box_faces(mid_boxes, 0)
        half_ghost = tuple(0.5 * (first + second) for first, second in zip(old_ghost, mid_ghost))
        in_use = slot_index < counts[strip_index]
        linked = links >= 0
        partner_base = (strip_index * PMAX, strip_index * PMAX,
                        ((strip_index - 1) % N_FINE) * PMAX, ((strip_index + 1) % N_FINE) * PMAX)
        partner_rows = [partner_base[facet_idx] + jnp.maximum(links[:, facet_idx], 0) for facet_idx in range(4)]

        def advance(blocked, level_faces):
            boundary = fine_faces(blocked)
            partner = (boundary[1], boundary[0], boundary[3], boundary[2])
            ghost_set = []
            for facet_idx in range(4):
                picked = jnp.take(partner[facet_idx], partner_rows[facet_idx], axis=0)
                ghost_set.append(jnp.where(linked[:, facet_idx][:, None, None, None], picked,
                                           spread(level_faces[facet_idx])))
            ghost_set.append(spread(level_faces[4]))
            ghost_set.append(spread(level_faces[5]))
            return blocked + 2.0 * coarse_rate * diffuse_cube(blocked, ghost_set), boundary

        start = patches.astype(jnp.float32)
        halfway_raw, first_bound = advance(start, old_ghost)
        halfway = lax.optimization_barrier(halfway_raw.astype(jnp.bfloat16)).astype(jnp.float32)
        final_raw, second_bound = advance(halfway, half_ghost)
        fine_out = jnp.where(in_use[:, None, None, None, None], final_raw, 0.0).astype(jnp.bfloat16)
        corrections = []
        for facet_idx in range(6):
            flux_sum = 2.0 * face_rate * (pooled(first_bound[facet_idx]) - 4.0 * old_ghost[facet_idx]
                                          + pooled(second_bound[facet_idx]) - 4.0 * half_ghost[facet_idx]) / 8.0
            correction = flux_sum - face_rate * (old_inner[facet_idx] - old_ghost[facet_idx])
            keep_mask = in_use & ~linked[:, facet_idx] if facet_idx < 4 else in_use
            corrections.append(jnp.where(keep_mask[:, None, None, None], correction, 0.0))
        grid_a = steps_h[None, :, None]
        grid_b = steps_h[None, None, :]
        slab_corr = jnp.zeros((NCOMP, half_len, NY, NX), jnp.float32)
        slab_corr = place_slab(slab_corr, grid_a, y_start[:, None, None] + grid_b,
                               ((x_start - 1) % NX)[:, None, None], corrections[0])
        slab_corr = place_slab(slab_corr, grid_a, y_start[:, None, None] + grid_b,
                               ((x_start + half_len) % NX)[:, None, None], corrections[1])
        slab_corr = place_slab(slab_corr, grid_a, ((y_start - 1) % NY)[:, None, None],
                               x_start[:, None, None] + grid_b, corrections[2])
        slab_corr = place_slab(slab_corr, grid_a, ((y_start + half_len) % NY)[:, None, None],
                               x_start[:, None, None] + grid_b, corrections[3])
        empty_plane = jnp.zeros((NCOMP, NY, NX), jnp.float32)
        low_plane = place_plane(empty_plane, y_start[:, None, None] + grid_a, x_start[:, None, None] + grid_b,
                                corrections[4])
        high_plane = place_plane(empty_plane, y_start[:, None, None] + grid_a, x_start[:, None, None] + grid_b,
                                 corrections[5])
        averaged = fine_out.astype(jnp.float32).reshape(
            row_slots, NCOMP, half_len, 2, half_len, 2, half_len, 2).sum(axis=(3, 5, 7)) / 8.0
        averaged = jnp.where(in_use[:, None, None, None, None], averaged, 0.0)
        shape_four = (row_slots, half_len, half_len, half_len)
        z_grid = jnp.broadcast_to(steps_h[None, :, None, None], shape_four)
        y_grid = jnp.broadcast_to(y_start[:, None, None, None] + steps_h[None, None, :, None], shape_four)
        x_grid = jnp.broadcast_to(x_start[:, None, None, None] + steps_h[None, None, None, :], shape_four)
        slab_avg = jnp.zeros((NCOMP, half_len, NY, NX), jnp.float32).at[:, z_grid, y_grid, x_grid].add(
            jnp.transpose(averaged, (1, 0, 2, 3, 4)))
        cover = jnp.zeros((N_FINE, FX), jnp.int32).at[strip_index, columns].add(in_use.astype(jnp.int32))
        return fine_out, slab_corr, low_plane, high_plane, slab_avg, cover

    fine_out, slab_corr, low_planes, high_planes, slab_avg, cover = lax.map(
        one_slab, (jnp.arange(N_OWN, dtype=jnp.int32), slab_fine, slab_columns, slab_counts, slab_links))
    slab_corr = slab_corr.at[:, :, -1].add(jnp.roll(low_planes, -1, axis=0))
    slab_corr = slab_corr.at[:, :, 0].add(jnp.roll(high_planes, 1, axis=0))

    def to_level(slabs):
        return jnp.transpose(slabs, (1, 0, 2, 3, 4)).reshape(NCOMP, NZ, NY, NX)

    covered = jnp.repeat(jnp.repeat(cover > 0, half_len, axis=1), half_len, axis=2)
    covered = jnp.repeat(covered, half_len, axis=0)[None]
    coarse_new = jnp.where(covered, to_level(slab_avg).astype(jnp.bfloat16),
                           (mid_level + to_level(slab_corr)).astype(jnp.bfloat16))
    fine_new = fine_out.reshape(SLOTS, NCOMP, edge_len, edge_len * edge_len)
    return coarse_new, fine_new
```

```python
import jax
import jax.numpy as jnp
from jax import lax
from jax.experimental import pallas as pl
from jax.experimental.pallas import tpu as pltpu
from jax.sharding import PartitionSpec as P

F32, BF16 = jnp.float32, jnp.bfloat16
SLOTS, COMPS, EDGE, HALF, LANES = 4, 5, 32, 16, 128
ROWS = COMPS * EDGE
CROWS = COMPS * HALF
CELLS = CROWS * HALF
PLANE = EDGE * EDGE
QUAD = 256

Y_NEAR, Y_NEXT, Y_ROW, Y_HALF, Y_FLUX, Y_COVER = 0, 80, 160, 320, 480, 560
Y_ROWS = 576
Z_NEAR, Z_NEXT, Z_FLUX, Z_LOW, Z_HIGH, Z_COVER = 0, 80, 160, 240, 256, 272
Z_ROWS = 288


def iota(shape, dim):
    return lax.broadcasted_iota(jnp.int32, shape, dim)


def ones_at(mask):
    return jnp.where(mask, 1.0, 0.0).astype(BF16)


def mm(left, right):
    return lax.dot_general(left, right, (((1,), (0,)), ((), ())), preferred_element_type=F32)


def chain(index, values):
    out = jnp.full(index.shape, values[-1], values[-1].dtype)
    for k in range(len(values) - 2, -1, -1):
        out = jnp.where(index == k, values[k], out)
    return out


class Tables:
    def __init__(self, col, cnt, nbr, rate):
        self.start = [col[s] * HALF for s in range(SLOTS)]
        self.used = [jnp.where(s < cnt[0], 1, 0) for s in range(SLOTS)]
        self.near = [[nbr[s, f] for s in range(SLOTS)] for f in range(4)]
        self.rate = [rate[c] for c in range(COMPS)]

    def rates(self, rows, per):
        return chain(iota((rows, LANES), 0) // per, self.rate)

    def packed(self, dim):
        n, x = iota((LANES, LANES), dim), iota((LANES, LANES), 1 - dim)
        return n // EDGE, n % EDGE, x

    def to_coarse(self, face):
        s, e, x = self.packed(0)
        hit = (x == chain(s, self.start) + e // 2) & (chain(s, self.used) > 0)
        if face is not None:
            hit = hit & (chain(s, self.near[face]) < 0)
        return ones_at(hit)

    def from_coarse(self, face, unlinked):
        s, e, x = self.packed(1)
        hit = x == chain(s, self.start) + e // 2
        if unlinked:
            hit = hit & (chain(s, self.near[face]) < 0)
        return ones_at(hit)

    def linked_lanes(self, face):
        s, e, n = self.packed(1)
        return ones_at(n == chain(s, self.near[face]) * EDGE + jnp.where(chain(s, self.near[face]) < 0, -LANES, e))

    def row_stencil(self):
        s, e, n = self.packed(1)
        low, high, x0 = chain(s, self.near[0]), chain(s, self.near[1]), chain(s, self.start)
        inside = (n // EDGE == s) & ((n % EDGE == e - 1) | (n % EDGE == e + 1))
        at_low = (e == 0) & (low >= 0) & (n == low * EDGE + EDGE - 1)
        at_high = (e == EDGE - 1) & (high >= 0) & (n == high * EDGE)
        left = (e == 0) & (low < 0) & (n == (x0 - 1) % LANES)
        right = (e == EDGE - 1) & (high < 0) & (n == (x0 + HALF) % LANES)
        return jnp.concatenate([ones_at(inside | at_low | at_high), ones_at(left | right)], axis=0)

    def side_pick(self):
        n, x = iota((LANES, LANES), 1), iota((LANES, LANES), 0)
        s, high = n // EDGE, n % EDGE >= HALF
        x0 = chain(s, self.start)
        spot = jnp.where(high, (x0 + HALF) % LANES, (x0 - 1) % LANES)
        open_face = jnp.where(high, chain(s, self.near[1]), chain(s, self.near[0])) < 0
        return ones_at((x == spot) & open_face)

    def pool_spread(self, mode):
        m, k = iota((SLOTS * LANES, QUAD), 0), iota((SLOTS * LANES, QUAD), 1)
        s, lane, x = m // LANES, m % LANES, k % LANES
        e, x0 = lane % EDGE, chain(s, self.start)
        hit = (lane // (2 * EDGE) == k // LANES) & (chain(s, self.used) > 0)
        if mode == 0:
            return ones_at(hit & (x == x0 + e // 2))
        left = (e == 0) & (chain(s, self.near[0]) < 0) & (x == (x0 - 1) % LANES)
        right = (e == EDGE - 1) & (chain(s, self.near[1]) < 0) & (x == (x0 + HALF) % LANES)
        return ones_at(hit & (left | right))


def copies(rows, per):
    out, src = iota((rows, rows // per), 0), iota((rows, rows // per), 1)
    return ones_at(out // per == src)


def pair_rows():
    out, src = iota((CROWS, ROWS), 0), iota((CROWS, ROWS), 1)
    return ones_at(src // 2 == out)


def z_stencil():
    out, src = iota((ROWS, ROWS), 0), iota((ROWS, ROWS), 1)
    same = out // EDGE == src // EDGE
    beside = same & ((src == out + 1) | (src == out - 1))
    return jnp.where(src == out, -6.0, jnp.where(beside, 1.0, 0.0)).astype(BF16)


def plane_stencil():
    m, n = iota((3 * QUAD, QUAD), 0), iota((3 * QUAD, QUAD), 1)
    e = n % EDGE
    own = (m < QUAD) & (
        ((m == n - 1) & (e > 0)) | ((m == n + 1) & (e < EDGE - 1)) | (m == n - EDGE) | (m == n + EDGE)
    )
    before = (m >= QUAD) & (m < QUAD + LANES) & (m - QUAD - LANES == n - EDGE)
    after = (m >= QUAD + LANES) & (m < 2 * QUAD) & (m - QUAD - LANES + QUAD == n + EDGE)
    p = m - 2 * QUAD
    partner = (m >= 2 * QUAD) & (
        ((e == 0) & (p == n + EDGE - 1)) | ((e == EDGE - 1) & (p == n - EDGE + 1))
    )
    return ones_at(own | before | after | partner)


def side_place(q):
    m, n = iota((LANES, QUAD), 0), iota((LANES, QUAD), 1)
    y, e = (n // EDGE + q * (QUAD // EDGE)) // 2, n % EDGE
    return ones_at((m < EDGE) & (m % HALF == y) & (e == jnp.where(m < HALF, 0, EDGE - 1)))


def partner_columns(load, tables, rows):
    lane = iota((rows, PLANE), 1) % EDGE
    at_low = jnp.where(lane == EDGE - 1, 1.0, 0.0).astype(BF16)
    at_high = jnp.where(lane == 0, 1.0, 0.0).astype(BF16)
    out = []
    for s in range(SLOTS):
        low, high = tables.near[0][s], tables.near[1][s]
        has_low = jnp.where(low >= 0, 1.0, 0.0).astype(BF16)
        has_high = jnp.where(high >= 0, 1.0, 0.0).astype(BF16)
        out.append(
            load(jnp.maximum(low, 0)) * (at_low * has_low) + load(jnp.maximum(high, 0)) * (at_high * has_high)
        )
    return out


def plane_terms(fields, partners, sides, q, weights):
    lo, hi = QUAD * q, QUAD * (q + 1)
    parts = []
    for s in range(SLOTS):
        field = fields[s]
        rows = field.shape[0]
        none = jnp.zeros((rows, LANES), BF16)
        parts.append(
            jnp.concatenate(
                [
                    field[:, lo:hi],
                    field[:, lo - LANES : lo] if q else none,
                    field[:, hi : hi + LANES] if q < 3 else none,
                    partners[s][:, lo:hi],
                    sides[s],
                ],
                axis=1,
            )
        )
    return mm(
        jnp.concatenate(parts, axis=0), jnp.concatenate([weights, side_place(q)], axis=0)
    )


def slot_sides(sides):
    return [sides if s == 0 else pltpu.roll(sides, LANES - EDGE * s, 1) for s in range(SLOTS)]


def edge_lanes(ghost, s, top):
    shift = (LANES - EDGE * (s + 1 if top else s)) % LANES
    moved = pltpu.roll(ghost, shift, 1) if shift else ghost
    lane = iota(ghost.shape, 1)
    kept = jnp.where(lane >= LANES - EDGE if top else lane < EDGE, moved, 0.0)
    none = jnp.zeros(ghost.shape, F32)
    return jnp.concatenate([none, kept] if top else [kept, none], axis=1)


def y_message_kernel(col, cnt, nbr, rate, low_ref, high_ref, coarse_ref, near_ref, far_ref, level):
    tables = Tables(col, cnt, nbr, rate)
    level[...] = coarse_ref[...].astype(F32)
    rates = tables.rates(ROWS, EDGE)
    coarse_rates = tables.rates(CROWS, HALF)
    stencil, rows_z, double, pairs = tables.row_stencil(), z_stencil(), copies(ROWS, 2), pair_rows()
    messages = []
    for top in (True, False):
        m, n = iota((SLOTS * LANES, QUAD), 0), iota((SLOTS * LANES, QUAD), 1)
        edge, inner = (LANES - EDGE, LANES - 2 * EDGE) if top else (0, EDGE)
        pack = ones_at(
            (m // LANES == n % LANES // EDGE)
            & (m % LANES == n % EDGE + jnp.where(n < LANES, edge, inner))
        )
        tile = high_ref if top else low_ref
        both = mm(jnp.concatenate([tile[s] for s in range(SLOTS)], axis=1), pack)
        row = both[:, :LANES].astype(BF16)
        near = level[pl.ds(HALF - 1 if top else 0, CROWS, stride=HALF), :]
        following = level[pl.ds(HALF - 2 if top else 1, CROWS, stride=HALF), :]
        near_fine = mm(double, near.astype(BF16)).astype(BF16)
        around = mm(jnp.concatenate([row, near_fine], axis=1), stencil) + mm(rows_z, row) + both[:, LANES:]
        half = (both[:, :LANES] + 2.0 * rates * around).astype(BF16)
        place = tables.to_coarse(3 if top else 2)
        sums = mm(pairs, jnp.concatenate([row, half], axis=1)).astype(BF16)
        cover = jnp.minimum(mm(jnp.ones((HALF, LANES), BF16), place), 1.0)
        flux = 0.25 * coarse_rates * mm(sums, jnp.concatenate([place, place], axis=0))
        flux = flux - coarse_rates * near * cover[:1]
        messages.append(
            (
                (Y_NEAR, near.astype(BF16)),
                (Y_NEXT, following.astype(BF16)),
                (Y_ROW, row),
                (Y_HALF, half),
                (Y_FLUX, flux.astype(BF16)),
                (Y_COVER, cover.astype(BF16)),
            )
        )
    even = lax.axis_index("fine") % 2 == 0
    up_ref_is_near = even

    @pl.when(up_ref_is_near)
    def _():
        for at, value in messages[0]:
            near_ref[at : at + value.shape[0], :] = value
        for at, value in messages[1]:
            far_ref[at : at + value.shape[0], :] = value

    @pl.when(jnp.logical_not(up_ref_is_near))
    def _():
        for at, value in messages[1]:
            near_ref[at : at + value.shape[0], :] = value
        for at, value in messages[0]:
            far_ref[at : at + value.shape[0], :] = value


def sort_arrivals(axis, near_ref, far_ref, arrived):
    even = lax.axis_index(axis) % 2 == 0

    @pl.when(even)
    def _():
        arrived[0] = far_ref[...]
        arrived[1] = near_ref[...]

    @pl.when(jnp.logical_not(even))
    def _():
        arrived[0] = near_ref[...]
        arrived[1] = far_ref[...]


PLANES = 16


def plane_rows(per, scale_inner):
    rows = COMPS * per
    out, src = iota((PLANES, rows), 0), iota((PLANES, rows), 1)
    c, last = out % 8, out >= 8
    edge = src == jnp.where(last, c * per + per - 1, c * per)
    real = c < COMPS
    if not scale_inner:
        return ones_at(edge & real)
    inner = src == jnp.where(last, c * per + per - 2, c * per + 1)
    return jnp.where(edge & real, -6.0, jnp.where(inner & real, 1.0, 0.0)).astype(BF16)


def z_message_kernel(
    col, cnt, nbr, rate, fine_ref, coarse_ref, y_near, y_far, near_ref, far_ref, arrived, planes, flux
):
    tables = Tables(col, cnt, nbr, rate)
    sort_arrivals("fine", y_near, y_far, arrived)
    picks = jnp.concatenate([plane_rows(EDGE, False), plane_rows(EDGE, True)], axis=0)
    inner = []
    for s in range(SLOTS):
        got = mm(picks, fine_ref[s])
        planes[s] = got[:PLANES].astype(BF16)
        inner.append(got[PLANES:])
    level = [
        [coarse_ref[pl.ds((c * HALF + z) * HALF, HALF), :] for c in range(COMPS)] for z in (0, 1, HALF - 2, HALF - 1)
    ]
    level = [jnp.concatenate(part, axis=0) for part in level]
    outer = jnp.concatenate([level[0], level[3]], axis=0)
    m, n = iota((2 * CROWS, LANES), 0), iota((2 * CROWS, LANES), 1)
    picked = jnp.where(m % HALF == n % HALF, mm(outer, tables.side_pick()), 0.0).astype(BF16)
    out, src = iota((PLANES, 2 * CROWS), 0), iota((PLANES, 2 * CROWS), 1)
    gather = ones_at((out // 8 == src // CROWS) & (out % 8 == src % CROWS // HALF))
    sides = slot_sides(mm(gather, picked))
    sides = [part.astype(BF16) for part in sides]
    fields = [planes[s] for s in range(SLOTS)]
    partners = partner_columns(lambda t: planes[t], tables, PLANES)
    fine_pick, coarse_pick = plane_rows(EDGE, False), plane_rows(HALF, False)
    ghosts, corners = [], []
    for k, face in ((0, 2), (1, 3)):
        row = mm(fine_pick, arrived[k, Y_ROW : Y_ROW + ROWS, :]).astype(BF16)
        corner = mm(coarse_pick, arrived[k, Y_NEAR : Y_NEAR + CROWS, :]).astype(BF16)
        corners.append(corner)
        ghosts.append(
            mm(
                jnp.concatenate([row, corner], axis=1),
                jnp.concatenate([tables.linked_lanes(face), tables.from_coarse(face, True)], axis=0),
            )
        )
    weights = plane_stencil()
    rates = chain(iota((PLANES, QUAD), 0) % 8, tables.rate + [jnp.zeros((), F32)] * 3)
    place = tables.pool_spread(0)
    for q in range(4):
        terms = plane_terms(fields, partners, sides, q, weights)
        summed = []
        for s in range(SLOTS):
            around = terms[PLANES * s : PLANES * (s + 1)] + inner[s][:, QUAD * q : QUAD * (q + 1)]
            if q == 0:
                around = around + edge_lanes(ghosts[0], s, False)
            if q == 3:
                around = around + edge_lanes(ghosts[1], s, True)
            field = fields[s][:, QUAD * q : QUAD * (q + 1)].astype(F32)
            summed.append((2.0 * field + 2.0 * rates * around).astype(BF16))
        for half in range(2):
            cells = mm(
                jnp.concatenate([part[:, LANES * half : LANES * (half + 1)] for part in summed], axis=1), place
            )
            y = 4 * q + 2 * half
            flux[pl.ds(y, PLANES, stride=HALF), :] = cells[:, :LANES]
            flux[pl.ds(y + 1, PLANES, stride=HALF), :] = cells[:, LANES:]
    cover = jnp.minimum(mm(jnp.ones((HALF, LANES), BF16), tables.to_coarse(None)), 1.0)
    coarse_rates = tables.rates(CROWS, HALF)
    messages = []
    for top in (True, False):
        near, following = (level[3], level[2]) if top else (level[0], level[1])
        at = 8 * HALF if top else 0
        total = 0.25 * coarse_rates * flux[at : at + CROWS, :] - coarse_rates * near.astype(F32) * cover[:1]
        messages.append(
            (
                (Z_NEAR, near),
                (Z_NEXT, following),
                (Z_FLUX, total.astype(BF16)),
                (Z_LOW, corners[0]),
                (Z_HIGH, corners[1]),
                (Z_COVER, cover.astype(BF16)),
            )
        )
    even = lax.axis_index("own") % 2 == 0

    @pl.when(even)
    def _():
        for at, value in messages[0]:
            near_ref[at : at + value.shape[0], :] = value
        for at, value in messages[1]:
            far_ref[at : at + value.shape[0], :] = value

    @pl.when(jnp.logical_not(even))
    def _():
        for at, value in messages[1]:
            near_ref[at : at + value.shape[0], :] = value
        for at, value in messages[0]:
            far_ref[at : at + value.shape[0], :] = value


SPAN = 32
DEEP = HALF + 2


def at_cell(c, z, y):
    return (c * DEEP + z + 1) * SPAN + 8 + y


def advance_kernel(
    col, cnt, nbr, rate, fine_ref, coarse_ref, y_near, y_far, z_near, z_far, coarse_out, fine_out,
    y_arr, z_arr, old, mean, half, split, average, outside,
):
    tables = Tables(col, cnt, nbr, rate)
    sort_arrivals("fine", y_near, y_far, y_arr)
    sort_arrivals("own", z_near, z_far, z_arr)
    for c in range(COMPS):
        for z in range(HALF):
            old[pl.ds(at_cell(c, z, 0), HALF), :] = coarse_ref[pl.ds((c * HALF + z) * HALF, HALF), :].astype(F32)
        for k, y in ((0, -1), (1, HALF)):
            at = Y_NEAR + c * HALF
            old[pl.ds(at_cell(c, 0, y), HALF, stride=SPAN), :] = y_arr[k, at : at + HALF, :].astype(F32)
        for k, z in ((0, -1), (1, HALF)):
            at = Z_NEAR + c * HALF
            old[pl.ds(at_cell(c, z, 0), HALF), :] = z_arr[k, at : at + HALF, :].astype(F32)
            row = c + (8 if k == 0 else 0)
            low = z_arr[k, Z_LOW : Z_LOW + HALF, :].astype(F32)
            high = z_arr[k, Z_HIGH : Z_HIGH + HALF, :].astype(F32)
            old[pl.ds(at_cell(c, z, -1), 1), :] = low[row : row + 1]
            old[pl.ds(at_cell(c, z, HALF), 1), :] = high[row : row + 1]

    def mixed(centre, total, r):
        total = total + pltpu.roll(centre, 1, 1) + pltpu.roll(centre, LANES - 1, 1)
        return centre + (0.5 * r) * (total - 6.0 * centre)

    for c in range(COMPS):
        r = tables.rate[c]
        for z in range(HALF):
            centre = old[pl.ds(at_cell(c, z, 0), HALF), :]
            total = (
                old[pl.ds(at_cell(c, z, -1), HALF), :]
                + old[pl.ds(at_cell(c, z, 1), HALF), :]
                + old[pl.ds(at_cell(c, z - 1, 0), HALF), :]
                + old[pl.ds(at_cell(c, z + 1, 0), HALF), :]
            )
            mean[pl.ds(at_cell(c, z, 0), HALF), :] = mixed(centre, total, r)
        for k, y, inside in ((0, -1, 0), (1, HALF, HALF - 1)):
            centre = old[pl.ds(at_cell(c, 0, y), HALF, stride=SPAN), :]
            at = Y_NEXT + c * HALF
            total = (
                y_arr[k, at : at + HALF, :].astype(F32)
                + old[pl.ds(at_cell(c, 0, inside), HALF, stride=SPAN), :]
                + old[pl.ds(at_cell(c, -1, y), HALF, stride=SPAN), :]
                + old[pl.ds(at_cell(c, 1, y), HALF, stride=SPAN), :]
            )
            mean[pl.ds(at_cell(c, 0, y), HALF, stride=SPAN), :] = mixed(centre, total, r)
        for k, z, inside in ((0, -1, 0), (1, HALF, HALF - 1)):
            centre = old[pl.ds(at_cell(c, z, 0), HALF), :]
            at = Z_NEXT + c * HALF
            total = (
                z_arr[k, at : at + HALF, :].astype(F32)
                + old[pl.ds(at_cell(c, inside, 0), HALF), :]
                + old[pl.ds(at_cell(c, z, -1), HALF), :]
                + old[pl.ds(at_cell(c, z, 1), HALF), :]
            )
            mean[pl.ds(at_cell(c, z, 0), HALF), :] = mixed(centre, total, r)

    rates = tables.rates(ROWS, EDGE)
    rates2 = 2.0 * jnp.concatenate([rates, rates], axis=1)
    weights, double = plane_stencil(), copies(ROWS, 2)
    out, src = iota((ROWS, 2 * CROWS), 0), iota((ROWS, 2 * CROWS), 1)
    end = jnp.where(src < CROWS, 0, EDGE - 1)
    rows_z = jnp.concatenate(
        [z_stencil(), ones_at((out % EDGE == end) & (out // EDGE == src % CROWS // HALF))], axis=1
    )
    pick = tables.side_pick()
    m, n = iota((CELLS, LANES), 0), iota((CELLS, LANES), 1)
    own_y = m % HALF == n % HALF
    picked = []
    for level in (old, mean):
        cells = jnp.concatenate(
            [level[pl.ds(at_cell(c, z, 0), HALF), :] for c in range(COMPS) for z in range(HALF)], axis=0
        ).astype(BF16)
        picked.append(jnp.where(own_y, mm(cells, pick), 0.0).astype(BF16))
    sides_both = mm(side_rows(), jnp.concatenate(picked, axis=1))

    linked = [tables.linked_lanes(2), tables.linked_lanes(3)]
    opened = [tables.from_coarse(2, True), tables.from_coarse(3, True)]
    window = tables.from_coarse(None, False)

    def level_row(level, y):
        rows = [level[pl.ds(at_cell(c, 0, y), HALF, stride=SPAN), :] for c in range(COMPS)]
        return mm(double, jnp.concatenate(rows, axis=0).astype(BF16)).astype(BF16)

    def ghost_planes(level):
        planes = []
        for z in (-1, HALF):
            planes += [level[pl.ds(at_cell(c, z, 0), HALF), :] for c in range(COMPS)]
        return mm(jnp.concatenate(planes, axis=0).astype(BF16), window)

    def substep(load, sides, ghosts, planes, finish):
        fields = [load(s) for s in range(SLOTS)]
        partners = partner_columns(load, tables, ROWS)
        sides = [part.astype(BF16) for part in slot_sides(sides)]
        spread = []
        for s in range(SLOTS):
            part = jnp.where(iota(planes.shape, 1) // EDGE == s, planes, 0.0)
            part = part + pltpu.roll(part, EDGE, 1)
            spread.append(part + pltpu.roll(part, 2 * EDGE, 1))
        m, n = iota((2 * CROWS, LANES), 0), iota((2 * CROWS, LANES), 1)
        for q in range(4):
            terms = plane_terms(fields, partners, sides, q, weights)
            for s in range(SLOTS):
                outer = []
                for k in (2 * q, 2 * q + 1):
                    outer.append(jnp.where(m % HALF == 2 * k + n // (2 * EDGE), spread[s], 0.0).astype(BF16))
                field = fields[s][:, QUAD * q : QUAD * (q + 1)]
                around = terms[ROWS * s : ROWS * (s + 1)] + mm(
                    rows_z, jnp.concatenate([field, jnp.concatenate(outer, axis=1)], axis=0)
                )
                if q == 0:
                    around = around + edge_lanes(ghosts[0], s, False)
                if q == 3:
                    around = around + edge_lanes(ghosts[1], s, True)
                finish(s, q, field.astype(F32) + rates2 * around)

    first = []
    for k, y in ((0, -1), (1, HALF)):
        row = y_arr[k, Y_ROW : Y_ROW + ROWS, :]
        first.append(
            mm(
                jnp.concatenate([row, level_row(old, y)], axis=1),
                jnp.concatenate([linked[k], opened[k]], axis=0),
            )
        )

    def keep_half(s, q, value):
        half[s, :, QUAD * q : QUAD * (q + 1)] = value.astype(BF16)

    substep(lambda s: fine_ref[s], sides_both[:, :LANES], first, ghost_planes(old), keep_half)

    out, src = iota((ROWS, 2 * PLANES), 0), iota((ROWS, 2 * PLANES), 1)
    low_end = (out % EDGE == 0) & (src == 8 + out // EDGE)
    high_end = (out % EDGE == EDGE - 1) & (src == PLANES + out // EDGE)
    ends = ones_at(low_end | high_end)
    second = []
    for k, y in ((0, -1), (1, HALF)):
        m, n = iota((SLOTS * LANES, LANES), 0), iota((SLOTS * LANES, LANES), 1)
        edge = LANES - EDGE if k else 0
        pack = ones_at((m // LANES == n // EDGE) & (m % LANES == n % EDGE + edge))
        tile = PLANE - LANES if k else 0
        mine = mm(jnp.concatenate([fine_ref[s, :, tile : tile + LANES] for s in range(SLOTS)], axis=1), pack)
        at = Z_HIGH if k else Z_LOW
        corner = jnp.concatenate([z_arr[0, at : at + PLANES, :], z_arr[1, at : at + PLANES, :]], axis=0)
        corner = mm(mm(ends, corner).astype(BF16), window)
        theirs = mm(y_arr[k, Y_HALF : Y_HALF + ROWS, :], linked[k]) + 2.0 * rates * (mine + corner)
        theirs = theirs.astype(BF16).astype(F32)
        is_linked = chain(iota((ROWS, LANES), 1) // EDGE, tables.near[2 + k]) >= 0
        second.append(jnp.where(is_linked, theirs, mm(level_row(mean, y), opened[k])))

    def keep_new(s, q, value):
        value = jnp.where(tables.used[s] > 0, value, 0.0)
        fine_out[s, :, QUAD * q : QUAD * (q + 1)] = value.astype(BF16)

    substep(lambda s: half[s], sides_both[:, LANES:], second, ghost_planes(mean), keep_new)

    into_cells, into_faces = tables.pool_spread(0), tables.pool_spread(1)
    faces_twice = jnp.concatenate([into_faces, into_faces], axis=0)
    for k in range(8):
        lanes = slice(LANES * k, LANES * (k + 1))
        new = jnp.concatenate([fine_out[s, :, lanes] for s in range(SLOTS)], axis=1)
        states = jnp.concatenate(
            [fine_ref[s, :, lanes] for s in range(SLOTS)] + [half[s, :, lanes] for s in range(SLOTS)], axis=1
        )
        cells, faces = mm(new, into_cells), mm(states, faces_twice)
        for i, value in enumerate((cells[:, :LANES], cells[:, LANES:], faces[:, :LANES], faces[:, LANES:])):
            split[i] = value
            pair = split[i, pl.ds(0, CROWS, stride=2), :] + split[i, pl.ds(1, CROWS, stride=2), :]
            target = average if i < 2 else outside
            target[pl.ds(2 * k + i % 2, CROWS, stride=HALF), :] = pair

    x = iota((HALF, LANES), 1)
    covered, left, right = x < 0, x < 0, x < 0
    for s in range(SLOTS):
        x0, used = tables.start[s], tables.used[s] > 0
        covered = covered | ((x >= x0) & (x < x0 + HALF) & used)
        left = left | ((x == (x0 - 1) % LANES) & used & (tables.near[0][s] < 0))
        right = right | ((x == (x0 + HALF) % LANES) & used & (tables.near[1][s] < 0))
    left, right = jnp.where(left, 1.0, 0.0), jnp.where(right, 1.0, 0.0)
    row = iota((HALF, LANES), 0)
    below = [jnp.where(row == (HALF - 1 if k else 0), y_arr[k, Y_COVER : Y_COVER + HALF, :].astype(F32), 0.0) for k in (0, 1)]
    ahead = [z_arr[k, Z_COVER : Z_COVER + HALF, :].astype(F32) for k in (0, 1)]
    for c in range(COMPS):
        r = tables.rate[c]
        for z in range(HALF):
            level0 = old[pl.ds(at_cell(c, z, 0), HALF), :]
            level1 = mean[pl.ds(at_cell(c, z, 0), HALF), :]
            line = pl.ds((c * HALF + z) * HALF, HALF)
            base = -r * level1
            change = 0.25 * r * outside[line, :] + (left + right) * base
            change = change - r * (left * pltpu.roll(level0, LANES - 1, 1) + right * pltpu.roll(level0, 1, 1))
            for k in (0, 1):
                whole = y_arr[k, Y_FLUX + c * HALF : Y_FLUX + (c + 1) * HALF, :].astype(F32)
                gain = base + (2.0 * r * r) * level0
                if z in (0, HALF - 1):
                    corner = old[pl.ds(at_cell(c, -1 if z == 0 else HALF, HALF if k else -1), 1), :]
                    gain = gain + (r * r) * corner
                one = row == (HALF - 1 if k else 0)
                change = change + jnp.where(one, whole[z : z + 1], 0.0) + below[k] * gain
            for k, edge in ((0, 0), (1, HALF - 1)):
                if z == edge:
                    flux = z_arr[k, Z_FLUX + c * HALF : Z_FLUX + (c + 1) * HALF, :].astype(F32)
                    change = change + flux + ahead[k] * (base + (2.0 * r * r) * level0)
            value = jnp.where(covered, 0.125 * average[line, :], 2.0 * level1 - level0 + change)
            coarse_out[line, :] = value.astype(BF16)


def side_rows():
    out, src = iota((ROWS, CELLS), 0), iota((ROWS, CELLS), 1)
    return ones_at(out // 2 == src // HALF)


SCALARS = [pl.BlockSpec(memory_space=pltpu.SMEM)] * 4
PARAMS = pltpu.CompilerParams(vmem_limit_bytes=48 * 1024 * 1024)


def whole():
    return pl.BlockSpec(memory_space=pltpu.VMEM)


def tile(lane):
    return pl.BlockSpec((SLOTS, ROWS, LANES), lambda i: (0, 0, lane))


def local(coarse_cells, fine_cells, diffusivity, patch_column, patch_count, neighbor_slot):
    fine = fine_cells.reshape(SLOTS, ROWS, PLANE)
    coarse = coarse_cells.reshape(CELLS, LANES)
    tables = (patch_column, patch_count, neighbor_slot, diffusivity)
    n_own, n_fine = lax.axis_size("own"), lax.axis_size("fine")

    def swap(value, axis, count, far):
        shift = 1 if far else 0
        pairs = []
        for i in range(count):
            partner = ((i - shift) ^ 1) + shift
            pairs.append((i, partner % count))
        return lax.ppermute(value, axis, pairs)

    y_shape = jax.ShapeDtypeStruct((Y_ROWS, LANES), BF16)
    y_near, y_far = pl.pallas_call(
        y_message_kernel,
        grid=(1,),
        in_specs=SCALARS + [tile(0), tile(7), pl.BlockSpec((CELLS, LANES), lambda i: (0, 0))],
        out_specs=[pl.BlockSpec((Y_ROWS, LANES), lambda i: (0, 0))] * 2,
        out_shape=[y_shape] * 2,
        scratch_shapes=[pltpu.VMEM((CELLS, LANES), F32)],
        compiler_params=PARAMS,
        name="y_messages",
    )(*tables, fine, fine, coarse)
    y_near, y_far = swap(y_near, "fine", n_fine, False), swap(y_far, "fine", n_fine, True)

    z_shape = jax.ShapeDtypeStruct((Z_ROWS, LANES), BF16)
    z_near, z_far = pl.pallas_call(
        z_message_kernel,
        in_specs=SCALARS + [whole()] * 4,
        out_specs=[whole()] * 2,
        out_shape=[z_shape] * 2,
        scratch_shapes=[
            pltpu.VMEM((2, Y_ROWS, LANES), BF16),
            pltpu.VMEM((SLOTS, PLANES, PLANE), BF16),
            pltpu.VMEM((PLANES * HALF, LANES), F32),
        ],
        compiler_params=PARAMS,
        name="z_messages",
    )(*tables, fine, coarse, y_near, y_far)
    z_near, z_far = swap(z_near, "own", n_own, False), swap(z_far, "own", n_own, True)

    coarse_new, fine_new = pl.pallas_call(
        advance_kernel,
        in_specs=SCALARS + [whole()] * 6,
        out_specs=[whole()] * 2,
        out_shape=[
            jax.ShapeDtypeStruct((CELLS, LANES), BF16),
            jax.ShapeDtypeStruct((SLOTS, ROWS, PLANE), BF16),
        ],
        scratch_shapes=[
            pltpu.VMEM((2, Y_ROWS, LANES), BF16),
            pltpu.VMEM((2, Z_ROWS, LANES), BF16),
            pltpu.VMEM((COMPS * DEEP * SPAN, LANES), F32),
            pltpu.VMEM((COMPS * DEEP * SPAN, LANES), F32),
            pltpu.VMEM((SLOTS, ROWS, PLANE), BF16),
            pltpu.VMEM((4, ROWS, LANES), F32),
            pltpu.VMEM((CELLS, LANES), F32),
            pltpu.VMEM((CELLS, LANES), F32),
        ],
        compiler_params=PARAMS,
        name="advance",
    )(*tables, fine, coarse, y_near, y_far, z_near, z_far)
    return coarse_new.reshape(coarse_cells.shape), fine_new.reshape(fine_cells.shape)


def solution(mesh):
    return jax.shard_map(
        local,
        mesh=mesh,
        in_specs=(
            P(None, "own", "fine", None),
            P(("own", "fine"), None, None, None),
            P(),
            P(("own", "fine")),
            P(("own", "fine")),
            P(("own", "fine"), None),
        ),
        out_specs=(P(None, "own", "fine", None), P(("own", "fine"), None, None, None)),
        check_vma=False,
    )
```

```python
import functools

import jax
import jax.numpy as jnp
import numpy as np
from jax import lax
from jax.experimental import pallas as pl
from jax.experimental.pallas import tpu as pltpu
from jax.sharding import PartitionSpec as P

F32, BF16 = jnp.float32, jnp.bfloat16
SLOTS, COMPS, EDGE, HALF, LANES = 4, 5, 32, 16, 128
ROWS = COMPS * EDGE
CROWS = COMPS * HALF
CELLS = CROWS * HALF
PLANE = EDGE * EDGE
QUAD = 256

Y_NEAR, Y_NEXT, Y_ROW, Y_HALF, Y_FLUX, Y_COVER = 0, 80, 160, 320, 480, 560
Y_ROWS = 576
Z_NEAR, Z_NEXT, Z_FLUX, Z_LOW, Z_HIGH, Z_COVER = 0, 80, 160, 240, 256, 272
Z_ROWS = 288


def iota(shape, dim):
    return lax.broadcasted_iota(jnp.int32, shape, dim)


def ones_at(mask):
    return jnp.where(mask, 1.0, 0.0).astype(BF16)


def mm(left, right):
    return lax.dot_general(left, right, (((1,), (0,)), ((), ())), preferred_element_type=F32)


def chain(index, values):
    out = jnp.full(index.shape, values[-1], values[-1].dtype)
    for k in range(len(values) - 2, -1, -1):
        out = jnp.where(index == k, values[k], out)
    return out


class Tables:
    def __init__(self, col, cnt, nbr, rate):
        self.start = [col[s] * HALF for s in range(SLOTS)]
        self.used = [jnp.where(s < cnt[0], 1, 0) for s in range(SLOTS)]
        self.near = [[nbr[s, f] for s in range(SLOTS)] for f in range(4)]
        self.rate = [rate[c] for c in range(COMPS)]

    def rates(self, rows, per):
        return chain(iota((rows, LANES), 0) // per, self.rate)

    def packed(self, dim):
        n, x = iota((LANES, LANES), dim), iota((LANES, LANES), 1 - dim)
        return n // EDGE, n % EDGE, x

    def to_coarse(self, face):
        s, e, x = self.packed(0)
        hit = (x == chain(s, self.start) + e // 2) & (chain(s, self.used) > 0)
        if face is not None:
            hit = hit & (chain(s, self.near[face]) < 0)
        return ones_at(hit)

    def from_coarse(self, face, unlinked):
        s, e, x = self.packed(1)
        hit = x == chain(s, self.start) + e // 2
        if unlinked:
            hit = hit & (chain(s, self.near[face]) < 0)
        return ones_at(hit)

    def linked_lanes(self, face):
        s, e, n = self.packed(1)
        return ones_at(n == chain(s, self.near[face]) * EDGE + jnp.where(chain(s, self.near[face]) < 0, -LANES, e))

    def row_stencil(self):
        s, e, n = self.packed(1)
        low, high, x0 = chain(s, self.near[0]), chain(s, self.near[1]), chain(s, self.start)
        inside = (n // EDGE == s) & ((n % EDGE == e - 1) | (n % EDGE == e + 1))
        at_low = (e == 0) & (low >= 0) & (n == low * EDGE + EDGE - 1)
        at_high = (e == EDGE - 1) & (high >= 0) & (n == high * EDGE)
        left = (e == 0) & (low < 0) & (n == (x0 - 1) % LANES)
        right = (e == EDGE - 1) & (high < 0) & (n == (x0 + HALF) % LANES)
        return jnp.concatenate([ones_at(inside | at_low | at_high), ones_at(left | right)], axis=0)

    def side_pick(self):
        n, x = iota((LANES, LANES), 1), iota((LANES, LANES), 0)
        s, high = n // EDGE, n % EDGE >= HALF
        x0 = chain(s, self.start)
        spot = jnp.where(high, (x0 + HALF) % LANES, (x0 - 1) % LANES)
        open_face = jnp.where(high, chain(s, self.near[1]), chain(s, self.near[0])) < 0
        return ones_at((x == spot) & open_face)

    def pool_spread(self, mode):
        m, x = iota((SLOTS * LANES, LANES), 0), iota((SLOTS * LANES, LANES), 1)
        s, lane = m // LANES, m % LANES
        e, x0 = lane % EDGE, chain(s, self.start)
        if mode == 0:
            target = jnp.where(chain(s, self.used) > 0, x0 + e // 2, -1)
        else:
            low = [jnp.where((self.used[k] > 0) & (self.near[0][k] < 0), (self.start[k] - 1) % LANES, -1) for k in range(SLOTS)]
            high = [jnp.where((self.used[k] > 0) & (self.near[1][k] < 0), (self.start[k] + HALF) % LANES, -1) for k in range(SLOTS)]
            target = jnp.where(e == 0, chain(s, low), jnp.where(e == EDGE - 1, chain(s, high), -1))
        first = lane < 2 * EDGE
        hit = x == target
        return jnp.concatenate([ones_at(hit & first), ones_at(hit & jnp.logical_not(first))], axis=1)


def copies(rows, per):
    out, src = iota((rows, rows // per), 0), iota((rows, rows // per), 1)
    return ones_at(out // per == src)


def pair_rows():
    out, src = iota((CROWS, ROWS), 0), iota((CROWS, ROWS), 1)
    return ones_at(src // 2 == out)


def z_stencil():
    out, src = iota((ROWS, ROWS), 0), iota((ROWS, ROWS), 1)
    same = out // EDGE == src // EDGE
    beside = same & ((src == out + 1) | (src == out - 1))
    return jnp.where(src == out, -6.0, jnp.where(beside, 1.0, 0.0)).astype(BF16)


def grid_of(rows, columns):
    return np.indices((rows, columns))


def plane_stencil():
    m, n = grid_of(3 * QUAD, QUAD)
    e = n % EDGE
    own = (m < QUAD) & (
        ((m == n - 1) & (e > 0)) | ((m == n + 1) & (e < EDGE - 1)) | (m == n - EDGE) | (m == n + EDGE)
    )
    before = (m >= QUAD) & (m < QUAD + LANES) & (m - QUAD - LANES == n - EDGE)
    after = (m >= QUAD + LANES) & (m < 2 * QUAD) & (m - QUAD - LANES + QUAD == n + EDGE)
    p = m - 2 * QUAD
    partner = (m >= 2 * QUAD) & (
        ((e == 0) & (p == n + EDGE - 1)) | ((e == EDGE - 1) & (p == n - EDGE + 1))
    )
    return own | before | after | partner


def side_place(q):
    m, n = grid_of(LANES, QUAD)
    y, e = (n // EDGE + q * (QUAD // EDGE)) // 2, n % EDGE
    return (m < EDGE) & (m % HALF == y) & (e == np.where(m < HALF, 0, EDGE - 1))


def plane_weights():
    return np.concatenate([plane_stencil()] + [side_place(q) for q in range(4)]).astype(BF16)


def side_rows():
    out, src = grid_of(ROWS, CELLS)
    return (out // 2 == src // HALF).astype(BF16)


def partner_columns(load, tables, rows):
    lane = iota((rows, PLANE), 1) % EDGE
    at_low = jnp.where(lane == EDGE - 1, 1.0, 0.0).astype(BF16)
    at_high = jnp.where(lane == 0, 1.0, 0.0).astype(BF16)
    out = []
    for s in range(SLOTS):
        low, high = tables.near[0][s], tables.near[1][s]
        has_low = jnp.where(low >= 0, 1.0, 0.0).astype(BF16)
        has_high = jnp.where(high >= 0, 1.0, 0.0).astype(BF16)
        out.append(
            load(jnp.maximum(low, 0)) * (at_low * has_low) + load(jnp.maximum(high, 0)) * (at_high * has_high)
        )
    return out


def plane_terms(fields, partners, sides, q, weights):
    lo, hi = QUAD * q, QUAD * (q + 1)
    parts = []
    for s in range(SLOTS):
        field = fields[s]
        rows = field.shape[0]
        none = jnp.zeros((rows, LANES), BF16)
        parts.append(
            jnp.concatenate(
                [
                    field[:, lo:hi],
                    field[:, lo - LANES : lo] if q else none,
                    field[:, hi : hi + LANES] if q < 3 else none,
                    partners[s][:, lo:hi],
                    sides[s],
                ],
                axis=1,
            )
        )
    place = 3 * QUAD + LANES * q
    table = jnp.concatenate([weights[: 3 * QUAD, :], weights[place : place + LANES, :]], axis=0)
    return mm(jnp.concatenate(parts, axis=0), table)


def slot_sides(sides):
    return [sides if s == 0 else pltpu.roll(sides, LANES - EDGE * s, 1) for s in range(SLOTS)]


def edge_lanes(ghost, s, top):
    shift = (LANES - EDGE * (s + 1 if top else s)) % LANES
    moved = pltpu.roll(ghost, shift, 1) if shift else ghost
    lane = iota(ghost.shape, 1)
    kept = jnp.where(lane >= LANES - EDGE if top else lane < EDGE, moved, 0.0)
    none = jnp.zeros(ghost.shape, F32)
    return jnp.concatenate([none, kept] if top else [kept, none], axis=1)


def y_message_kernel(
    col_hbm, cnt_hbm, nbr_hbm, rate_hbm, fine_hbm, coarse_hbm, near_ref, far_ref,
    col, cnt, nbr, rate, low_ref, high_ref, coarse_ref, level, packs, rows_z, sems,
):
    fetches = [
        pltpu.make_async_copy(source, target, sems.at[i])
        for i, (source, target) in enumerate(
            (
                (col_hbm, col),
                (cnt_hbm, cnt),
                (nbr_hbm, nbr),
                (rate_hbm, rate),
                (coarse_hbm, coarse_ref),
                (fine_hbm.at[:, :, 0:LANES], low_ref),
                (fine_hbm.at[:, :, PLANE - LANES : PLANE], high_ref),
            )
        )
    ]
    for fetch in fetches:
        fetch.start()
    m, n = iota((SLOTS * LANES, QUAD), 0), iota((SLOTS * LANES, QUAD), 1)
    for i, (edge, inner) in enumerate(((0, EDGE), (LANES - EDGE, LANES - 2 * EDGE))):
        packs[i] = ones_at(
            (m // LANES == n % LANES // EDGE) & (m % LANES == n % EDGE + jnp.where(n < LANES, edge, inner))
        )
    rows_z[...] = z_stencil()
    for fetch in fetches:
        fetch.wait()
    tables = Tables(col, cnt, nbr, rate)
    level[...] = coarse_ref[...].astype(F32)
    rates = tables.rates(ROWS, EDGE)
    coarse_rates = tables.rates(CROWS, HALF)
    stencil, double, pairs = tables.row_stencil(), copies(ROWS, 2), pair_rows()
    messages = []
    for top in (True, False):
        tile = high_ref if top else low_ref
        both = mm(jnp.concatenate([tile[s] for s in range(SLOTS)], axis=1), packs[int(top)])
        row = both[:, :LANES].astype(BF16)
        near = level[pl.ds(HALF - 1 if top else 0, CROWS, stride=HALF), :]
        following = level[pl.ds(HALF - 2 if top else 1, CROWS, stride=HALF), :]
        near_fine = mm(double, near.astype(BF16)).astype(BF16)
        around = mm(jnp.concatenate([row, near_fine], axis=1), stencil) + mm(rows_z[...], row) + both[:, LANES:]
        half = (both[:, :LANES] + 2.0 * rates * around).astype(BF16)
        place = tables.to_coarse(3 if top else 2)
        sums = mm(pairs, jnp.concatenate([row, half], axis=1)).astype(BF16)
        cover = jnp.minimum(mm(jnp.ones((HALF, LANES), BF16), place), 1.0)
        flux = 0.25 * coarse_rates * mm(sums, jnp.concatenate([place, place], axis=0))
        flux = flux - coarse_rates * near * cover[:1]
        messages.append(
            (
                (Y_NEAR, near.astype(BF16)),
                (Y_NEXT, following.astype(BF16)),
                (Y_ROW, row),
                (Y_HALF, half),
                (Y_FLUX, flux.astype(BF16)),
                (Y_COVER, cover.astype(BF16)),
            )
        )
    store_by_parity("fine", near_ref, far_ref, *messages)


def sort_arrivals(axis, near_ref, far_ref, arrived):
    even = lax.axis_index(axis) % 2 == 0

    @pl.when(even)
    def _():
        arrived[0] = far_ref[...]
        arrived[1] = near_ref[...]

    @pl.when(jnp.logical_not(even))
    def _():
        arrived[0] = near_ref[...]
        arrived[1] = far_ref[...]


PLANES = 16


def plane_rows(per, scale_inner):
    rows = COMPS * per
    out, src = iota((PLANES, rows), 0), iota((PLANES, rows), 1)
    c, last = out % 8, out >= 8
    edge = src == jnp.where(last, c * per + per - 1, c * per)
    real = c < COMPS
    if not scale_inner:
        return ones_at(edge & real)
    inner = src == jnp.where(last, c * per + per - 2, c * per + 1)
    return jnp.where(edge & real, -6.0, jnp.where(inner & real, 1.0, 0.0)).astype(BF16)


def store_by_parity(axis, near_ref, far_ref, up, down):
    even = lax.axis_index(axis) % 2 == 0

    @pl.when(even)
    def _():
        for at, value in up:
            near_ref[at : at + value.shape[0], :] = value
        for at, value in down:
            far_ref[at : at + value.shape[0], :] = value

    @pl.when(jnp.logical_not(even))
    def _():
        for at, value in down:
            near_ref[at : at + value.shape[0], :] = value
        for at, value in up:
            far_ref[at : at + value.shape[0], :] = value


def coarse_planes(coarse_ref, zs):
    return jnp.concatenate(
        [coarse_ref[pl.ds((c * HALF + z) * HALF, HALF), :] for z in zs for c in range(COMPS)], axis=0
    )


def interior_kernel(
    col, cnt, nbr, rate, fine_ref, coarse_ref, weights, side_sum, half_ref, edges_ref, planes_ref, flux_ref, place_ref,
    flux, summed, split,
):
    tables = Tables(col, cnt, nbr, rate)
    m, n = iota((CELLS, LANES), 0), iota((CELLS, LANES), 1)
    picked = jnp.where(m % HALF == n % HALF, mm(coarse_ref[...], tables.side_pick()), 0.0).astype(BF16)
    sides = [part.astype(BF16) for part in slot_sides(mm(side_sum[...], picked))]
    fields = [fine_ref[s] for s in range(SLOTS)]
    partners = partner_columns(lambda t: fine_ref[t], tables, ROWS)
    rows_z = z_stencil()
    rates = tables.rates(ROWS, EDGE)
    rates2 = 2.0 * jnp.concatenate([rates, rates], axis=1)
    place_ref[...] = tables.pool_spread(0)
    summed[...] = jnp.zeros(summed.shape, F32)
    planes_ref[...] = jnp.zeros(planes_ref.shape, F32)
    for q in range(4):
        lanes = slice(QUAD * q, QUAD * (q + 1))
        terms = plane_terms(fields, partners, sides, q, weights)
        for s in range(SLOTS):
            field = fields[s][:, lanes]
            start = field.astype(F32)
            value = start + rates2 * (terms[ROWS * s : ROWS * (s + 1)] + mm(rows_z, field))
            half_ref[s, :, lanes] = value.astype(BF16)
            if q == 0:
                edges_ref[s, :, :LANES] = value[:, :LANES]
            if q == 3:
                edges_ref[s, :, LANES:] = value[:, LANES:]
            both = value + start
            for h in range(2):
                part = slice(LANES * h, LANES * (h + 1))
                at = slice(QUAD * q + LANES * h, QUAD * q + LANES * (h + 1))
                split[2 * h] = value[:, part]
                split[2 * h + 1] = both[:, part]
                for p in range(2):
                    first = (EDGE - 1) * p
                    planes_ref[s, 8 * p : 8 * p + COMPS, at] = split[2 * h, pl.ds(first, COMPS, stride=EDGE), :]
                    row = PLANES * (2 * q + h) + 8 * p
                    summed[row : row + COMPS, LANES * s : LANES * (s + 1)] = (
                        split[2 * h + 1, pl.ds(first, COMPS, stride=EDGE), :]
                    )
    cells = mm(summed[...].astype(BF16), place_ref[...])
    for k in range(8):
        part = cells[PLANES * k : PLANES * (k + 1)]
        flux[pl.ds(2 * k, PLANES, stride=HALF), :] = part[:, :LANES]
        flux[pl.ds(2 * k + 1, PLANES, stride=HALF), :] = part[:, LANES:]
    cover = jnp.minimum(mm(jnp.ones((HALF, LANES), BF16), tables.to_coarse(None)), 1.0)
    coarse_rates = tables.rates(CROWS, HALF)
    for p in range(2):
        near = coarse_planes(coarse_ref, ((HALF - 1) * p,)).astype(F32)
        total = 0.25 * coarse_rates * flux[8 * HALF * p : 8 * HALF * p + CROWS, :]
        flux_ref[CROWS * p : CROWS * (p + 1), :] = total - coarse_rates * near * cover[:1]


def z_message_kernel(col, cnt, nbr, rate, coarse_ref, flux_in, y_near, y_far, near_ref, far_ref, arrived, flux):
    tables = Tables(col, cnt, nbr, rate)
    sort_arrivals("fine", y_near, y_far, arrived)
    flux[...] = flux_in[...]
    fine_pick, coarse_pick = plane_rows(EDGE, False), plane_rows(HALF, False)
    place = tables.to_coarse(None)
    rates = chain(iota((PLANES, LANES), 0) % 8, tables.rate + [jnp.zeros((), F32)] * 3)
    corners = []
    for k, face in ((0, 2), (1, 3)):
        row = mm(fine_pick, arrived[k, Y_ROW : Y_ROW + ROWS, :]).astype(BF16)
        corner = mm(coarse_pick, arrived[k, Y_NEAR : Y_NEAR + CROWS, :]).astype(BF16)
        corners.append(corner)
        ghost = mm(
            jnp.concatenate([row, corner], axis=1),
            jnp.concatenate([tables.linked_lanes(face), tables.from_coarse(face, True)], axis=0),
        )
        gain = (0.5 * rates * rates) * mm(ghost.astype(BF16), place)
        for p in range(2):
            at = pl.ds(CROWS * p + (HALF - 1) * k, COMPS, stride=HALF)
            flux[at, :] = flux[at, :] + gain[8 * p : 8 * p + COMPS]
    cover = jnp.minimum(mm(jnp.ones((HALF, LANES), BF16), place), 1.0).astype(BF16)
    messages = []
    for top in (True, False):
        near, following = (HALF - 1, HALF - 2) if top else (0, 1)
        messages.append(
            (
                (Z_NEAR, coarse_planes(coarse_ref, (near,))),
                (Z_NEXT, coarse_planes(coarse_ref, (following,))),
                (Z_FLUX, flux[CROWS * top : CROWS * (top + 1), :].astype(BF16)),
                (Z_LOW, corners[0]),
                (Z_HIGH, corners[1]),
                (Z_COVER, cover),
            )
        )
    store_by_parity("own", near_ref, far_ref, *messages)


SPAN = 32
DEEP = HALF + 2


def at_cell(c, z, y):
    return (c * DEEP + z + 1) * SPAN + 8 + y


def mixed(centre, total, r):
    total = total + pltpu.roll(centre, 1, 1) + pltpu.roll(centre, LANES - 1, 1)
    return centre + (0.5 * r) * (total - 6.0 * centre)


def own_mean(old, mean, tables, zs):
    for c in range(COMPS):
        for z in zs:
            total = (
                old[pl.ds(at_cell(c, z, -1), HALF), :]
                + old[pl.ds(at_cell(c, z, 1), HALF), :]
                + old[pl.ds(at_cell(c, z - 1, 0), HALF), :]
                + old[pl.ds(at_cell(c, z + 1, 0), HALF), :]
            )
            mean[pl.ds(at_cell(c, z, 0), HALF), :] = mixed(
                old[pl.ds(at_cell(c, z, 0), HALF), :], total, tables.rate[c]
            )


def strip_mean(old, mean, y_arr, tables):
    for c in range(COMPS):
        for k, y, inside in ((0, -1, 0), (1, HALF, HALF - 1)):
            at = Y_NEXT + c * HALF
            total = (
                y_arr[k, at : at + HALF, :].astype(F32)
                + old[pl.ds(at_cell(c, 0, inside), HALF, stride=SPAN), :]
                + old[pl.ds(at_cell(c, -1, y), HALF, stride=SPAN), :]
                + old[pl.ds(at_cell(c, 1, y), HALF, stride=SPAN), :]
            )
            mean[pl.ds(at_cell(c, 0, y), HALF, stride=SPAN), :] = mixed(
                old[pl.ds(at_cell(c, 0, y), HALF, stride=SPAN), :], total, tables.rate[c]
            )


def fill_old(old, coarse_ref, y_arr, zs):
    for c in range(COMPS):
        for z in zs:
            old[pl.ds(at_cell(c, z, 0), HALF), :] = coarse_ref[pl.ds((c * HALF + z) * HALF, HALF), :].astype(F32)
        for k, y in ((0, -1), (1, HALF)):
            at = Y_NEAR + c * HALF
            old[pl.ds(at_cell(c, 0, y), HALF, stride=SPAN), :] = y_arr[k, at : at + HALF, :].astype(F32)


def neighbour_rows(fine_ref, k):
    m, n = iota((SLOTS * LANES, LANES), 0), iota((SLOTS * LANES, LANES), 1)
    edge = LANES - EDGE if k else 0
    pack = ones_at((m // LANES == n // EDGE) & (m % LANES == n % EDGE + edge))
    tile = PLANE - LANES if k else 0
    return mm(jnp.concatenate([fine_ref[s, :, tile : tile + LANES] for s in range(SLOTS)], axis=1), pack)


class CoarseLanes:
    def __init__(self, tables, y_arr):
        x = iota((HALF, LANES), 1)
        covered, left, right = x < 0, x < 0, x < 0
        for s in range(SLOTS):
            x0, used = tables.start[s], tables.used[s] > 0
            covered = covered | ((x >= x0) & (x < x0 + HALF) & used)
            left = left | ((x == (x0 - 1) % LANES) & used & (tables.near[0][s] < 0))
            right = right | ((x == (x0 + HALF) % LANES) & used & (tables.near[1][s] < 0))
        self.covered = covered
        self.left, self.right = jnp.where(left, 1.0, 0.0), jnp.where(right, 1.0, 0.0)
        self.sides = self.left + self.right
        self.beside = [y_arr[k, Y_COVER : Y_COVER + HALF, :].astype(F32)[:1] for k in (0, 1)]

    def update(self, r, level0, level1, average, change):
        low, high = pltpu.roll(level0, LANES - 1, 1), pltpu.roll(level0, 1, 1)
        change = change - r * (self.sides * level1 + self.left * low + self.right * high)
        return jnp.where(self.covered, 0.125 * average, 2.0 * level1 - level0 + change).astype(BF16)

    def beyond_y(self, k, r, level0, level1, flux, corner):
        gain = (2.0 * r * r) * level0 - r * level1
        if corner is not None:
            gain = gain + (r * r) * corner
        return flux + self.beside[k] * gain


def middle_kernel(early, *refs):
    is_early = lax.axis_index("own") == 0

    @pl.when(is_early if early else jnp.logical_not(is_early))
    def _():
        middle_body(*(refs if early else refs[:14] + refs[20:]))

    if not early:

        @pl.when(is_early)
        def _():
            for done, out in zip(refs[14:20], refs[20:26]):
                out[...] = done[...]


def middle_body(
    col, cnt, nbr, rate, fine_ref, coarse_ref, y_near, y_far, half_in, edges_ref, planes_in, weights, side_sum, place_ref,
    coarse_out, fine_out, rows_ref, planes_ref, theirs_ref, faces_ref,
    half, y_arr, old, mean, split, average, outside, pairs,
):
    tables = Tables(col, cnt, nbr, rate)
    sort_arrivals("fine", y_near, y_far, y_arr)
    fill_old(old, coarse_ref, y_arr, range(HALF))
    for c in range(COMPS):
        for z in (-1, HALF):
            old[pl.ds(at_cell(c, z, 0) - 8, SPAN), :] = jnp.zeros((SPAN, LANES), F32)
    own_mean(old, mean, tables, range(HALF))
    strip_mean(old, mean, y_arr, tables)
    rates = tables.rates(ROWS, EDGE)
    rates2 = 2.0 * jnp.concatenate([rates, rates], axis=1)
    double, rows_z = copies(ROWS, 2), z_stencil()
    cells = jnp.concatenate(
        [mean[pl.ds(at_cell(c, z, 0), HALF), :] for c in range(COMPS) for z in range(HALF)], axis=0
    ).astype(BF16)
    m, n = iota((CELLS, LANES), 0), iota((CELLS, LANES), 1)
    picked = jnp.where(m % HALF == n % HALF, mm(cells, tables.side_pick()), 0.0).astype(BF16)
    sides = [part.astype(BF16) for part in slot_sides(mm(side_sum[...], picked))]

    def level_row(level, y):
        rows = [level[pl.ds(at_cell(c, 0, y), HALF, stride=SPAN), :] for c in range(COMPS)]
        return mm(double, jnp.concatenate(rows, axis=0).astype(BF16)).astype(BF16)

    half[...] = half_in[...]
    planes_ref[...] = planes_in[...]
    second = []
    plane_rates = chain(iota((PLANES, LANES), 0) % 8, tables.rate + [jnp.zeros((), F32)] * 3)
    for k, y in ((0, -1), (1, HALF)):
        linked, opened = tables.linked_lanes(2 + k), tables.from_coarse(2 + k, True)
        row = y_arr[k, Y_ROW : Y_ROW + ROWS, :]
        ghost = mm(jnp.concatenate([row, level_row(old, y)], axis=1), jnp.concatenate([linked, opened], axis=0))
        plane_ghost = mm(plane_rows(EDGE, False), ghost.astype(BF16))
        tile = slice(PLANE - LANES, PLANE) if k else slice(0, LANES)
        part = slice(LANES * k, LANES * (k + 1))
        for s in range(SLOTS):
            add = edge_lanes(ghost, s, bool(k))[:, part]
            half[s, :, tile] = (edges_ref[s, :, part] + 2.0 * rates * add).astype(BF16)
            add = edge_lanes(plane_ghost, s, bool(k))[:, part]
            planes_ref[s, :, tile] = planes_ref[s, :, tile] + 2.0 * plane_rates * add
        theirs = mm(y_arr[k, Y_HALF : Y_HALF + ROWS, :], linked) + 2.0 * rates * neighbour_rows(fine_ref, k)
        theirs_ref[k] = theirs
        theirs = theirs.astype(BF16).astype(F32)
        is_linked = chain(iota((ROWS, LANES), 1) // EDGE, tables.near[2 + k]) >= 0
        second.append(jnp.where(is_linked, theirs, mm(level_row(mean, y), opened)))

    rows_ref[...] = jnp.zeros(rows_ref.shape, F32)
    fields = [half[s] for s in range(SLOTS)]
    partners = partner_columns(lambda t: half[t], tables, ROWS)
    for q in range(4):
        lanes = slice(QUAD * q, QUAD * (q + 1))
        terms = plane_terms(fields, partners, sides, q, weights)
        for s in range(SLOTS):
            field = fields[s][:, lanes]
            around = terms[ROWS * s : ROWS * (s + 1)] + mm(rows_z, field)
            if q == 0:
                around = around + edge_lanes(second[0], s, False)
            if q == 3:
                around = around + edge_lanes(second[1], s, True)
            start = field.astype(F32)
            for h in range(2):
                split[h, :ROWS, :] = start[:, LANES * h : LANES * (h + 1)]
                split[h, ROWS : 2 * ROWS, :] = (
                    split[h, :ROWS, :] + fine_ref[s, :, QUAD * q + LANES * h : QUAD * q + LANES * (h + 1)].astype(F32)
                )
                pairs[2 * q + h, :, LANES * s : LANES * (s + 1)] = (
                    split[h, pl.ds(ROWS, CROWS, stride=2), :] + split[h, pl.ds(ROWS + 1, CROWS, stride=2), :]
                ).astype(BF16)
                at = slice(QUAD * q + LANES * h, QUAD * q + LANES * (h + 1))
                for w, first in enumerate((1, 2, EDGE - 3, EDGE - 2)):
                    rows_ref[s, 8 * w : 8 * w + COMPS, at] = split[h, pl.ds(first, COMPS, stride=EDGE), :]
            value = jnp.where(tables.used[s] > 0, start + rates2 * around, 0.0)
            fine_out[s, :, lanes] = value.astype(BF16)

    faces = mm(pairs[...].reshape(8 * CROWS, SLOTS * LANES), tables.pool_spread(1))
    tall = jnp.concatenate(
        [
            jnp.concatenate([fine_out[s, :, LANES * k : LANES * (k + 1)] for s in range(SLOTS)], axis=1)
            for k in range(8)
        ],
        axis=0,
    )
    cells = mm(tall, place_ref[...])
    coarse_rates = tables.rates(CROWS, HALF)
    scale = 0.25 * coarse_rates
    for j in range(2):
        lanes = slice(LANES * j, LANES * (j + 1))
        split[j] = cells[:, lanes]
        for k in range(8):
            at = pl.ds(2 * k + j, CROWS, stride=HALF)
            outside[at, :] = scale * faces[CROWS * k : CROWS * (k + 1), lanes]
            average[at, :] = (
                split[j, pl.ds(ROWS * k, CROWS, stride=2), :] + split[j, pl.ds(ROWS * k + 1, CROWS, stride=2), :]
            )
    for c in range(COMPS):
        for p in range(2):
            at = CROWS * p + HALF * c
            faces_ref[at : at + HALF, :] = outside[pl.ds((c * HALF + (HALF - 1) * p) * HALF, HALF), :]

    masks = CoarseLanes(tables, y_arr)

    def strip(level, y):
        return jnp.concatenate([level[pl.ds(at_cell(c, 0, y), HALF, stride=SPAN), :] for c in range(COMPS)], axis=0)

    for k, y in ((0, 0), (1, HALF - 1)):
        at = pl.ds(y, CROWS, stride=HALF)
        flux = y_arr[k, Y_FLUX : Y_FLUX + CROWS, :].astype(F32)
        outside[at, :] = outside[at, :] + masks.beyond_y(k, coarse_rates, strip(old, y), strip(mean, y), flux, None)
    for c in range(COMPS):
        for z in range(HALF):
            line = pl.ds((c * HALF + z) * HALF, HALF)
            if z in (0, HALF - 1):
                coarse_out[line, :] = jnp.zeros((HALF, LANES), BF16)
                continue
            coarse_out[line, :] = masks.update(
                tables.rate[c], old[pl.ds(at_cell(c, z, 0), HALF), :], mean[pl.ds(at_cell(c, z, 0), HALF), :],
                average[line, :], outside[line, :],
            )


NEAR = 32


def last_kernel(
    col, cnt, nbr, rate, coarse_ref, y_near, y_far, z_near, z_far, weights, place_ref,
    coarse_in, fine_in, rows_ref, planes_ref, theirs_ref, faces_ref,
    coarse_out, fine_hbm, y_arr, z_arr, old, mean, near, split, following, spread, ghost, level_rows, put, fine_out, sems,
):
    tables = Tables(col, cnt, nbr, rate)
    sort_arrivals("fine", y_near, y_far, y_arr)
    sort_arrivals("own", z_near, z_far, z_arr)
    fill_old(old, coarse_ref, y_arr, (0, 1, HALF - 2, HALF - 1))
    for k in (0, 1):
        following[k] = y_arr[k, Y_NEXT : Y_NEXT + CROWS, :].astype(F32)
    for c in range(COMPS):
        for k, z in ((0, -1), (1, HALF)):
            at = Z_NEAR + c * HALF
            old[pl.ds(at_cell(c, z, 0), HALF), :] = z_arr[k, at : at + HALF, :].astype(F32)
    by_comp = DEEP * SPAN
    for k, z in ((0, -1), (1, HALF)):
        first = 0 if k else 8
        low = z_arr[k, Z_LOW : Z_LOW + HALF, :].astype(F32)
        high = z_arr[k, Z_HIGH : Z_HIGH + HALF, :].astype(F32)
        old[pl.ds(at_cell(0, z, -1), COMPS, stride=by_comp), :] = low[first : first + COMPS]
        old[pl.ds(at_cell(0, z, HALF), COMPS, stride=by_comp), :] = high[first : first + COMPS]
    own_mean(old, mean, tables, (0, HALF - 1))
    comp_rates = chain(iota((COMPS, LANES), 0), tables.rate)
    level_rows[...] = jnp.zeros(level_rows.shape, F32)
    for k, y, inside in ((0, -1, 0), (1, HALF, HALF - 1)):
        for p, z in ((0, 0), (1, HALF - 1)):
            total = (
                following[k, pl.ds(z, COMPS, stride=HALF), :]
                + old[pl.ds(at_cell(0, z, inside), COMPS, stride=by_comp), :]
                + old[pl.ds(at_cell(0, z - 1, y), COMPS, stride=by_comp), :]
                + old[pl.ds(at_cell(0, z + 1, y), COMPS, stride=by_comp), :]
            )
            value = mixed(old[pl.ds(at_cell(0, z, y), COMPS, stride=by_comp), :], total, comp_rates)
            for w in (2 * p, 2 * p + 1):
                level_rows[k, 8 * w : 8 * w + COMPS, :] = value
    for c in range(COMPS):
        for k, z, inside in ((0, -1, 0), (1, HALF, HALF - 1)):
            at = Z_NEXT + c * HALF
            total = (
                z_arr[k, at : at + HALF, :].astype(F32)
                + old[pl.ds(at_cell(c, inside, 0), HALF), :]
                + old[pl.ds(at_cell(c, z, -1), HALF), :]
                + old[pl.ds(at_cell(c, z, 1), HALF), :]
            )
            mean[pl.ds(at_cell(c, z, 0), HALF), :] = mixed(
                old[pl.ds(at_cell(c, z, 0), HALF), :], total, tables.rate[c]
            )

    window = tables.from_coarse(None, False)
    n = iota((2 * CROWS, LANES), 1)

    def planes_of(level, zs):
        return jnp.concatenate([level[pl.ds(at_cell(c, z, 0), HALF), :] for z in zs for c in range(COMPS)], axis=0)

    first_y = iota((COMPS, LANES), 1) < 2 * EDGE

    def ghost_rows(level, i):
        planes = mm(planes_of(level, (-1, HALF)).astype(BF16), window)
        for s in range(SLOTS):
            part = jnp.where(n // EDGE == s, planes, 0.0)
            part = part + pltpu.roll(part, EDGE, 1)
            spread[s] = part + pltpu.roll(part, 2 * EDGE, 1)
            for k in range(8):
                for p in range(2):
                    even = spread[s, pl.ds(CROWS * p + 2 * k, COMPS, stride=HALF), :]
                    odd = spread[s, pl.ds(CROWS * p + 2 * k + 1, COMPS, stride=HALF), :]
                    ghost[i, s, 8 * p : 8 * p + COMPS, LANES * k : LANES * (k + 1)] = jnp.where(first_y, even, odd)

    ghost[...] = jnp.zeros(ghost.shape, F32)
    ghost_rows(old, 0)
    ghost_rows(mean, 1)
    rates = chain(iota((NEAR, LANES), 0) % 8, tables.rate + [jnp.zeros((), F32)] * 3)
    rates2 = 2.0 * jnp.concatenate([rates, rates], axis=1)
    wide = 2.0 * chain(iota((2 * 8, PLANE), 0) % 8, tables.rate + [jnp.zeros((), F32)] * 3)

    along = []
    for s in range(SLOTS):
        ends = (planes_ref[s] + wide * ghost[0, s]).astype(BF16).astype(F32)
        one, two, next_last, last = (rows_ref[s, 8 * w : 8 * (w + 1), :] for w in range(4))
        near[s] = jnp.concatenate([ends[:8], one, last, ends[8:]], axis=0).astype(BF16)
        along.append(
            jnp.concatenate(
                [
                    one - 6.0 * ends[:8] + ghost[1, s, :8],
                    ends[:8] + two - 6.0 * one,
                    ends[8:] + next_last - 6.0 * last,
                    last - 6.0 * ends[8:] + ghost[1, s, 8:],
                ],
                axis=0,
            )
        )

    m = iota((2 * CROWS, LANES), 0)
    picked = jnp.where(
        m % HALF == n % HALF, mm(planes_of(mean, (0, HALF - 1)).astype(BF16), tables.side_pick()), 0.0
    ).astype(BF16)
    out, src = iota((NEAR, 2 * CROWS), 0), iota((NEAR, 2 * CROWS), 1)
    side_sum = ones_at((out % 8 == src % CROWS // HALF) & (out % 8 < COMPS) & (out // 16 == src // CROWS))
    sides = [part.astype(BF16) for part in slot_sides(mm(side_sum, picked))]
    ghosts = []
    zero = jnp.zeros((8, LANES), F32)
    for k in (0, 1):
        at = Z_HIGH if k else Z_LOW
        corner = jnp.concatenate([z_arr[0, at : at + PLANES, :], z_arr[1, at : at + PLANES, :]], axis=0)
        corner = mm(corner, window)
        for w, first in enumerate((0, 1, EDGE - 2, EDGE - 1)):
            level_rows[2, 8 * w : 8 * w + COMPS, :] = theirs_ref[k, pl.ds(first, COMPS, stride=EDGE), :]
        theirs = level_rows[2] + 2.0 * rates * jnp.concatenate([corner[8:16], zero, zero, corner[16:24]], axis=0)
        theirs = theirs.astype(BF16).astype(F32)
        is_linked = chain(iota((NEAR, LANES), 1) // EDGE, tables.near[2 + k]) >= 0
        level = mm(level_rows[k].astype(BF16), tables.from_coarse(2 + k, True))
        ghosts.append(jnp.where(is_linked, theirs, level))
    fields = [near[s] for s in range(SLOTS)]
    partners = partner_columns(lambda t: near[t], tables, NEAR)
    fresh = []
    for q in range(4):
        lanes = slice(QUAD * q, QUAD * (q + 1))
        terms = plane_terms(fields, partners, sides, q, weights)
        for s in range(SLOTS):
            field = fields[s][:, lanes]
            around = terms[NEAR * s : NEAR * (s + 1)] + along[s][:, lanes]
            if q == 0:
                around = around + edge_lanes(ghosts[0], s, False)
            if q == 3:
                around = around + edge_lanes(ghosts[1], s, True)
            value = jnp.where(tables.used[s] > 0, field.astype(F32) + rates2 * around, 0.0).astype(BF16)
            fresh.append(value)
            value = value.astype(F32)
            for h in range(2):
                for w, first in enumerate((0, 1, EDGE - 2, EDGE - 1)):
                    put[s, 2 * q + h, pl.ds(first, COMPS, stride=EDGE), :] = (
                        value[8 * w : 8 * w + COMPS, LANES * h : LANES * (h + 1)]
                    )
    a = iota((ROWS, LANES), 0) % EDGE
    replaced = (a < 2) | (a >= EDGE - 2)
    sends = []
    for s in range(SLOTS):
        for k in range(8):
            lanes = slice(LANES * k, LANES * (k + 1))
            fine_out[s, :, lanes] = jnp.where(replaced, put[s, k], fine_in[s, :, lanes].astype(F32)).astype(BF16)
        sends.append(pltpu.make_async_copy(fine_out.at[s], fine_hbm.at[s], sems.at[s]))
        sends[s].start()

    tall = jnp.concatenate(
        [
            jnp.concatenate([fresh[SLOTS * q + s][:, LANES * h : LANES * (h + 1)] for s in range(SLOTS)], axis=1)
            for q in range(4)
            for h in range(2)
        ],
        axis=0,
    )
    cells = mm(tall, place_ref[...])
    for k in range(8):
        part = cells[NEAR * k : NEAR * (k + 1)]
        for j in range(2):
            lane = slice(LANES * j, LANES * (j + 1))
            for p in range(2):
                pair = part[16 * p : 16 * p + 8, lane] + part[16 * p + 8 : 16 * p + 16, lane]
                split[pl.ds(8 * HALF * p + 2 * k + j, 8, stride=HALF), :] = pair

    coarse_out[...] = coarse_in[...]
    masks = CoarseLanes(tables, y_arr)
    row = iota((HALF, LANES), 0)
    for c in range(COMPS):
        r = tables.rate[c]
        y_flux = [y_arr[k, Y_FLUX + c * HALF : Y_FLUX + (c + 1) * HALF, :].astype(F32) for k in (0, 1)]
        for p, z in ((0, 0), (1, HALF - 1)):
            beyond = -1 if z == 0 else HALF
            level0, level1 = old[pl.ds(at_cell(c, z, 0), HALF), :], mean[pl.ds(at_cell(c, z, 0), HALF), :]
            halo = old[pl.ds(at_cell(c, beyond, 0), HALF), :]
            halo = masks.left * pltpu.roll(halo, LANES - 1, 1) + masks.right * pltpu.roll(halo, 1, 1)
            at = CROWS * p + HALF * c
            change = faces_ref[at : at + HALF, :] + (r * r) * halo
            for k, y in ((0, 0), (1, HALF - 1)):
                corner = old[pl.ds(at_cell(c, beyond, HALF if k else -1), 1), :]
                extra = masks.beyond_y(k, r, level0[y : y + 1], level1[y : y + 1], y_flux[k][z : z + 1], corner)
                change = change + jnp.where(row == y, extra, 0.0)
            flux = z_arr[p, Z_FLUX + c * HALF : Z_FLUX + (c + 1) * HALF, :].astype(F32)
            ahead = z_arr[p, Z_COVER : Z_COVER + HALF, :].astype(F32)
            change = change + flux + ahead * ((2.0 * r * r) * level0 - r * level1)
            coarse_out[pl.ds((c * HALF + z) * HALF, HALF), :] = masks.update(
                r, level0, level1, split[pl.ds(8 * HALF * p + c * HALF, HALF), :], change
            )
    for send in sends:
        send.wait()


SCALARS = [pl.BlockSpec(memory_space=pltpu.SMEM)] * 4
PARAMS = pltpu.CompilerParams(vmem_limit_bytes=32 * 1024 * 1024)
FETCH_PARAMS = pltpu.CompilerParams(vmem_limit_bytes=60 * 1024 * 1024)


def whole():
    return pl.BlockSpec(memory_space=pltpu.VMEM)


def local(coarse_cells, fine_cells, diffusivity, patch_column, patch_count, neighbor_slot):
    fine = fine_cells.reshape(SLOTS, ROWS, PLANE)
    coarse = coarse_cells.reshape(CELLS, LANES)
    tables = (patch_column, patch_count, neighbor_slot, diffusivity)
    n_own, n_fine = lax.axis_size("own"), lax.axis_size("fine")

    def swap(value, axis, count, far):
        shift = 1 if far else 0
        pairs = []
        for i in range(count):
            partner = ((i - shift) ^ 1) + shift
            pairs.append((i, partner % count))
        return lax.ppermute(value, axis, pairs)

    y_shape = jax.ShapeDtypeStruct((Y_ROWS, LANES), BF16)
    field_shape = jax.ShapeDtypeStruct((SLOTS, ROWS, PLANE), BF16)
    cells_shape = jax.ShapeDtypeStruct((CELLS, LANES), BF16)
    y_near, y_far = pl.pallas_call(
        y_message_kernel,
        in_specs=[pl.BlockSpec(memory_space=pl.ANY)] * 6,
        out_specs=[whole()] * 2,
        out_shape=[y_shape] * 2,
        scratch_shapes=[
            pltpu.SMEM((SLOTS,), jnp.int32),
            pltpu.SMEM((1,), jnp.int32),
            pltpu.SMEM((SLOTS, 4), jnp.int32),
            pltpu.SMEM((COMPS,), F32),
            pltpu.VMEM((SLOTS, ROWS, LANES), BF16),
            pltpu.VMEM((SLOTS, ROWS, LANES), BF16),
            pltpu.VMEM((CELLS, LANES), BF16),
            pltpu.VMEM((CELLS, LANES), F32),
            pltpu.VMEM((2, SLOTS * LANES, QUAD), BF16),
            pltpu.VMEM((ROWS, ROWS), BF16),
            pltpu.SemaphoreType.DMA((7,)),
        ],
        compiler_params=FETCH_PARAMS,
        name="y_messages",
    )(*tables, fine, coarse)
    y_near, y_far = swap(y_near, "fine", n_fine, False), swap(y_far, "fine", n_fine, True)

    planes_shape = jax.ShapeDtypeStruct((SLOTS, PLANES, PLANE), F32)
    level = pltpu.VMEM((COMPS * DEEP * SPAN, LANES), F32)
    weights, side_sum = jnp.asarray(plane_weights()), jnp.asarray(side_rows())
    half, edges, planes, flux, place = pl.pallas_call(
        interior_kernel,
        in_specs=SCALARS + [whole()] * 4,
        out_specs=[whole()] * 5,
        out_shape=[
            field_shape,
            jax.ShapeDtypeStruct((SLOTS, ROWS, QUAD), F32),
            planes_shape,
            jax.ShapeDtypeStruct((2 * CROWS, LANES), F32),
            jax.ShapeDtypeStruct((SLOTS * LANES, QUAD), BF16),
        ],
        scratch_shapes=[
            pltpu.VMEM((PLANES * HALF, LANES), F32),
            pltpu.VMEM((8 * PLANES, SLOTS * LANES), F32),
            pltpu.VMEM((4, ROWS, LANES), F32),
        ],
        compiler_params=PARAMS,
        cost_estimate=pl.CostEstimate(flops=2_000_000_000, bytes_accessed=5_000_000, transcendentals=0),
        name="interior",
    )(*tables, fine, coarse, weights, side_sum)

    z_shape = jax.ShapeDtypeStruct((Z_ROWS, LANES), BF16)
    z_near, z_far = pl.pallas_call(
        z_message_kernel,
        in_specs=SCALARS + [whole()] * 4,
        out_specs=[whole()] * 2,
        out_shape=[z_shape] * 2,
        scratch_shapes=[pltpu.VMEM((2, Y_ROWS, LANES), BF16), pltpu.VMEM((2 * CROWS, LANES), F32)],
        compiler_params=PARAMS,
        name="z_messages",
    )(*tables, coarse, flux, y_near, y_far)
    parts_shape = [
        cells_shape,
        field_shape,
        jax.ShapeDtypeStruct((SLOTS, 32, PLANE), F32),
        planes_shape,
        jax.ShapeDtypeStruct((2, ROWS, LANES), F32),
        jax.ShapeDtypeStruct((2 * CROWS, LANES), F32),
    ]
    middle_args = (*tables, fine, coarse, y_near, y_far, half, edges, planes, weights, side_sum, place)

    def middle(early, *parts):
        return pl.pallas_call(
            functools.partial(middle_kernel, early),
            in_specs=SCALARS + [whole()] * (10 + len(parts)),
            out_specs=[whole()] * 6,
            out_shape=parts_shape,
            scratch_shapes=[
                pltpu.VMEM((SLOTS, ROWS, PLANE), BF16),
                pltpu.VMEM((2, Y_ROWS, LANES), BF16),
                level,
                level,
                pltpu.VMEM((2, CELLS, LANES), F32),
                pltpu.VMEM((CELLS, LANES), F32),
                pltpu.VMEM((CELLS, LANES), F32),
                pltpu.VMEM((8, CROWS, SLOTS * LANES), BF16),
            ],
            compiler_params=PARAMS,
            cost_estimate=pl.CostEstimate(flops=3_000_000_000, bytes_accessed=8_000_000, transcendentals=0),
            name="middle_early" if early else "middle_late",
        )(*middle_args, *parts)

    z_near = swap(z_near, "own", n_own, False)
    parts = middle(True)
    z_far, parts = lax.optimization_barrier((z_far, parts))
    z_far = swap(z_far, "own", n_own, True)
    parts = middle(False, *parts)

    coarse_new, fine_new = pl.pallas_call(
        last_kernel,
        in_specs=SCALARS + [whole()] * 13,
        out_specs=[whole(), pl.BlockSpec(memory_space=pl.ANY)],
        out_shape=[cells_shape, field_shape],
        scratch_shapes=[
            pltpu.VMEM((2, Y_ROWS, LANES), BF16),
            pltpu.VMEM((2, Z_ROWS, LANES), BF16),
            level,
            level,
            pltpu.VMEM((SLOTS, 32, PLANE), BF16),
            pltpu.VMEM((PLANES * HALF, LANES), F32),
            pltpu.VMEM((2, CROWS, LANES), F32),
            pltpu.VMEM((SLOTS, 2 * CROWS, LANES), F32),
            pltpu.VMEM((2, SLOTS, PLANES, PLANE), F32),
            pltpu.VMEM((3, 32, LANES), F32),
            pltpu.VMEM((SLOTS, 8, ROWS, LANES), F32),
            pltpu.VMEM((SLOTS, ROWS, PLANE), BF16),
            pltpu.SemaphoreType.DMA((SLOTS,)),
        ],
        compiler_params=PARAMS,
        name="last",
    )(*tables, coarse, y_near, y_far, z_near, z_far, weights, place, *parts)
    return coarse_new.reshape(coarse_cells.shape), fine_new.reshape(fine_cells.shape)


def solution(mesh):
    return jax.shard_map(
        local,
        mesh=mesh,
        in_specs=(
            P(None, "own", "fine", None),
            P(("own", "fine"), None, None, None),
            P(),
            P(("own", "fine")),
            P(("own", "fine")),
            P(("own", "fine"), None),
        ),
        out_specs=(P(None, "own", "fine", None), P(("own", "fine"), None, None, None)),
        check_vma=False,
    )
```

```python
import functools

import jax
import jax.numpy as jnp
import numpy as np
from jax import lax
from jax.experimental import pallas as pl
from jax.experimental.pallas import tpu as pltpu
from jax.sharding import PartitionSpec as P

F32, BF16 = jnp.float32, jnp.bfloat16
SLOTS, COMPS, EDGE, HALF, LANES = 4, 5, 32, 16, 128
ROWS = COMPS * EDGE
CROWS = COMPS * HALF
CELLS = CROWS * HALF
PLANE = EDGE * EDGE
QUAD = 256

Y_NEAR, Y_NEXT, Y_ROW, Y_HALF, Y_FLUX, Y_COVER = 0, 80, 160, 320, 480, 560
Y_ROWS = 576
Z_NEAR, Z_NEXT, Z_FLUX, Z_LOW, Z_HIGH, Z_COVER = 0, 80, 160, 240, 256, 272
Z_ROWS = 288


def iota(shape, dim):
    return lax.broadcasted_iota(jnp.int32, shape, dim)


def ones_at(mask):
    return jnp.where(mask, 1.0, 0.0).astype(BF16)


def mm(left, right):
    return lax.dot_general(left, right, (((1,), (0,)), ((), ())), preferred_element_type=F32)


def chain(index, values):
    out = jnp.full(index.shape, values[-1], values[-1].dtype)
    for k in range(len(values) - 2, -1, -1):
        out = jnp.where(index == k, values[k], out)
    return out


class Tables:
    def __init__(self, col, cnt, nbr, rate):
        self.start = [col[s] * HALF for s in range(SLOTS)]
        self.used = [jnp.where(s < cnt[0], 1, 0) for s in range(SLOTS)]
        self.near = [[nbr[s, f] for s in range(SLOTS)] for f in range(4)]
        self.rate = [rate[c] for c in range(COMPS)]

    def rates(self, rows, per):
        return chain(iota((rows, LANES), 0) // per, self.rate)

    def packed(self, dim):
        n, x = iota((LANES, LANES), dim), iota((LANES, LANES), 1 - dim)
        return n // EDGE, n % EDGE, x

    def to_coarse(self, face):
        s, e, x = self.packed(0)
        hit = (x == chain(s, self.start) + e // 2) & (chain(s, self.used) > 0)
        if face is not None:
            hit = hit & (chain(s, self.near[face]) < 0)
        return ones_at(hit)

    def from_coarse(self, face, unlinked):
        s, e, x = self.packed(1)
        hit = x == chain(s, self.start) + e // 2
        if unlinked:
            hit = hit & (chain(s, self.near[face]) < 0)
        return ones_at(hit)

    def linked_lanes(self, face):
        s, e, n = self.packed(1)
        return ones_at(n == chain(s, self.near[face]) * EDGE + jnp.where(chain(s, self.near[face]) < 0, -LANES, e))

    def row_stencil(self):
        s, e, n = self.packed(1)
        low, high, x0 = chain(s, self.near[0]), chain(s, self.near[1]), chain(s, self.start)
        inside = (n // EDGE == s) & ((n % EDGE == e - 1) | (n % EDGE == e + 1))
        at_low = (e == 0) & (low >= 0) & (n == low * EDGE + EDGE - 1)
        at_high = (e == EDGE - 1) & (high >= 0) & (n == high * EDGE)
        left = (e == 0) & (low < 0) & (n == (x0 - 1) % LANES)
        right = (e == EDGE - 1) & (high < 0) & (n == (x0 + HALF) % LANES)
        return jnp.concatenate([ones_at(inside | at_low | at_high), ones_at(left | right)], axis=0)

    def side_pick(self):
        n, x = iota((LANES, LANES), 1), iota((LANES, LANES), 0)
        s, high = n // EDGE, n % EDGE >= HALF
        x0 = chain(s, self.start)
        spot = jnp.where(high, (x0 + HALF) % LANES, (x0 - 1) % LANES)
        open_face = jnp.where(high, chain(s, self.near[1]), chain(s, self.near[0])) < 0
        return ones_at((x == spot) & open_face)

    def pool_spread(self, mode):
        m, x = iota((SLOTS * LANES, LANES), 0), iota((SLOTS * LANES, LANES), 1)
        s, lane = m // LANES, m % LANES
        e, x0 = lane % EDGE, chain(s, self.start)
        if mode == 0:
            target = jnp.where(chain(s, self.used) > 0, x0 + e // 2, -1)
        else:
            low = [jnp.where((self.used[k] > 0) & (self.near[0][k] < 0), (self.start[k] - 1) % LANES, -1) for k in range(SLOTS)]
            high = [jnp.where((self.used[k] > 0) & (self.near[1][k] < 0), (self.start[k] + HALF) % LANES, -1) for k in range(SLOTS)]
            target = jnp.where(e == 0, chain(s, low), jnp.where(e == EDGE - 1, chain(s, high), -1))
        first = lane < 2 * EDGE
        hit = x == target
        return jnp.concatenate([ones_at(hit & first), ones_at(hit & jnp.logical_not(first))], axis=1)


def copies(rows, per):
    out, src = iota((rows, rows // per), 0), iota((rows, rows // per), 1)
    return ones_at(out // per == src)


def pair_rows():
    out, src = iota((CROWS, ROWS), 0), iota((CROWS, ROWS), 1)
    return ones_at(src // 2 == out)


def z_stencil():
    out, src = iota((ROWS, ROWS), 0), iota((ROWS, ROWS), 1)
    same = out // EDGE == src // EDGE
    beside = same & ((src == out + 1) | (src == out - 1))
    return jnp.where(src == out, -6.0, jnp.where(beside, 1.0, 0.0)).astype(BF16)


def grid_of(rows, columns):
    return np.indices((rows, columns))


def plane_stencil():
    m, n = grid_of(3 * QUAD, QUAD)
    e = n % EDGE
    own = (m < QUAD) & (
        ((m == n - 1) & (e > 0)) | ((m == n + 1) & (e < EDGE - 1)) | (m == n - EDGE) | (m == n + EDGE)
    )
    before = (m >= QUAD) & (m < QUAD + LANES) & (m - QUAD - LANES == n - EDGE)
    after = (m >= QUAD + LANES) & (m < 2 * QUAD) & (m - QUAD - LANES + QUAD == n + EDGE)
    p = m - 2 * QUAD
    partner = (m >= 2 * QUAD) & (
        ((e == 0) & (p == n + EDGE - 1)) | ((e == EDGE - 1) & (p == n - EDGE + 1))
    )
    return own | before | after | partner


def side_place(q):
    m, n = grid_of(LANES, QUAD)
    y, e = (n // EDGE + q * (QUAD // EDGE)) // 2, n % EDGE
    return (m < EDGE) & (m % HALF == y) & (e == np.where(m < HALF, 0, EDGE - 1))


def plane_weights():
    return np.concatenate([plane_stencil()] + [side_place(q) for q in range(4)]).astype(BF16)


def side_rows():
    out, src = grid_of(ROWS, CELLS)
    return (out // 2 == src // HALF).astype(BF16)


def partner_columns(load, tables, rows):
    lane = iota((rows, PLANE), 1) % EDGE
    at_low = jnp.where(lane == EDGE - 1, 1.0, 0.0).astype(BF16)
    at_high = jnp.where(lane == 0, 1.0, 0.0).astype(BF16)
    out = []
    for s in range(SLOTS):
        low, high = tables.near[0][s], tables.near[1][s]
        has_low = jnp.where(low >= 0, 1.0, 0.0).astype(BF16)
        has_high = jnp.where(high >= 0, 1.0, 0.0).astype(BF16)
        out.append(
            load(jnp.maximum(low, 0)) * (at_low * has_low) + load(jnp.maximum(high, 0)) * (at_high * has_high)
        )
    return out


def plane_terms(fields, partners, sides, q, weights):
    lo, hi = QUAD * q, QUAD * (q + 1)
    parts = []
    for s in range(SLOTS):
        field = fields[s]
        rows = field.shape[0]
        none = jnp.zeros((rows, LANES), BF16)
        parts.append(
            jnp.concatenate(
                [
                    field[:, lo:hi],
                    field[:, lo - LANES : lo] if q else none,
                    field[:, hi : hi + LANES] if q < 3 else none,
                    partners[s][:, lo:hi],
                    sides[s],
                ],
                axis=1,
            )
        )
    place = 3 * QUAD + LANES * q
    table = jnp.concatenate([weights[: 3 * QUAD, :], weights[place : place + LANES, :]], axis=0)
    return mm(jnp.concatenate(parts, axis=0), table)


def slot_sides(sides):
    return [sides if s == 0 else pltpu.roll(sides, LANES - EDGE * s, 1) for s in range(SLOTS)]


def edge_lanes(ghost, s, top):
    shift = (LANES - EDGE * (s + 1 if top else s)) % LANES
    moved = pltpu.roll(ghost, shift, 1) if shift else ghost
    lane = iota(ghost.shape, 1)
    kept = jnp.where(lane >= LANES - EDGE if top else lane < EDGE, moved, 0.0)
    none = jnp.zeros(ghost.shape, F32)
    return jnp.concatenate([none, kept] if top else [kept, none], axis=1)


def y_message_kernel(
    col_hbm, cnt_hbm, nbr_hbm, rate_hbm, fine_hbm, coarse_hbm, near_ref, far_ref,
    col, cnt, nbr, rate, low_ref, high_ref, coarse_ref, level, packs, rows_z, sems,
):
    fetches = [
        pltpu.make_async_copy(source, target, sems.at[i])
        for i, (source, target) in enumerate(
            (
                (col_hbm, col),
                (cnt_hbm, cnt),
                (nbr_hbm, nbr),
                (rate_hbm, rate),
                (coarse_hbm, coarse_ref),
                (fine_hbm.at[:, :, 0:LANES], low_ref),
                (fine_hbm.at[:, :, PLANE - LANES : PLANE], high_ref),
            )
        )
    ]
    for fetch in fetches:
        fetch.start()
    m, n = iota((SLOTS * LANES, QUAD), 0), iota((SLOTS * LANES, QUAD), 1)
    for i, (edge, inner) in enumerate(((0, EDGE), (LANES - EDGE, LANES - 2 * EDGE))):
        packs[i] = ones_at(
            (m // LANES == n % LANES // EDGE) & (m % LANES == n % EDGE + jnp.where(n < LANES, edge, inner))
        )
    rows_z[...] = z_stencil()
    for fetch in fetches:
        fetch.wait()
    tables = Tables(col, cnt, nbr, rate)
    level[...] = coarse_ref[...].astype(F32)
    rates = tables.rates(ROWS, EDGE)
    coarse_rates = tables.rates(CROWS, HALF)
    stencil, double, pairs = tables.row_stencil(), copies(ROWS, 2), pair_rows()
    messages = []
    for top in (True, False):
        tile = high_ref if top else low_ref
        both = mm(jnp.concatenate([tile[s] for s in range(SLOTS)], axis=1), packs[int(top)])
        row = both[:, :LANES].astype(BF16)
        near = level[pl.ds(HALF - 1 if top else 0, CROWS, stride=HALF), :]
        following = level[pl.ds(HALF - 2 if top else 1, CROWS, stride=HALF), :]
        near_fine = mm(double, near.astype(BF16)).astype(BF16)
        around = mm(jnp.concatenate([row, near_fine], axis=1), stencil) + mm(rows_z[...], row) + both[:, LANES:]
        half = (both[:, :LANES] + 2.0 * rates * around).astype(BF16)
        place = tables.to_coarse(3 if top else 2)
        sums = mm(pairs, jnp.concatenate([row, half], axis=1)).astype(BF16)
        cover = jnp.minimum(mm(jnp.ones((HALF, LANES), BF16), place), 1.0)
        flux = 0.25 * coarse_rates * mm(sums, jnp.concatenate([place, place], axis=0))
        flux = flux - coarse_rates * near * cover[:1]
        messages.append(
            (
                (Y_NEAR, near.astype(BF16)),
                (Y_NEXT, following.astype(BF16)),
                (Y_ROW, row),
                (Y_HALF, half),
                (Y_FLUX, flux.astype(BF16)),
                (Y_COVER, cover.astype(BF16)),
            )
        )
    store_by_parity("fine", near_ref, far_ref, *messages)


def sort_arrivals(axis, near_ref, far_ref, arrived):
    even = lax.axis_index(axis) % 2 == 0

    @pl.when(even)
    def _():
        arrived[0] = far_ref[...]
        arrived[1] = near_ref[...]

    @pl.when(jnp.logical_not(even))
    def _():
        arrived[0] = near_ref[...]
        arrived[1] = far_ref[...]


PLANES = 16


def plane_rows(per, scale_inner):
    rows = COMPS * per
    out, src = iota((PLANES, rows), 0), iota((PLANES, rows), 1)
    c, last = out % 8, out >= 8
    edge = src == jnp.where(last, c * per + per - 1, c * per)
    real = c < COMPS
    if not scale_inner:
        return ones_at(edge & real)
    inner = src == jnp.where(last, c * per + per - 2, c * per + 1)
    return jnp.where(edge & real, -6.0, jnp.where(inner & real, 1.0, 0.0)).astype(BF16)


def store_by_parity(axis, near_ref, far_ref, up, down):
    even = lax.axis_index(axis) % 2 == 0

    @pl.when(even)
    def _():
        for at, value in up:
            near_ref[at : at + value.shape[0], :] = value
        for at, value in down:
            far_ref[at : at + value.shape[0], :] = value

    @pl.when(jnp.logical_not(even))
    def _():
        for at, value in down:
            near_ref[at : at + value.shape[0], :] = value
        for at, value in up:
            far_ref[at : at + value.shape[0], :] = value


def coarse_planes(coarse_ref, zs):
    return jnp.concatenate(
        [coarse_ref[pl.ds((c * HALF + z) * HALF, HALF), :] for z in zs for c in range(COMPS)], axis=0
    )


def interior_kernel(
    col, cnt, nbr, rate, fine_ref, coarse_ref, weights, side_sum, half_ref, edges_ref, planes_ref, flux_ref, place_ref,
    flux, summed, split,
):
    tables = Tables(col, cnt, nbr, rate)
    m, n = iota((CELLS, LANES), 0), iota((CELLS, LANES), 1)
    picked = jnp.where(m % HALF == n % HALF, mm(coarse_ref[...], tables.side_pick()), 0.0).astype(BF16)
    sides = [part.astype(BF16) for part in slot_sides(mm(side_sum[...], picked))]
    fields = [fine_ref[s] for s in range(SLOTS)]
    partners = partner_columns(lambda t: fine_ref[t], tables, ROWS)
    rows_z = z_stencil()
    rates = tables.rates(ROWS, EDGE)
    rates2 = 2.0 * jnp.concatenate([rates, rates], axis=1)
    place_ref[...] = tables.pool_spread(0)
    summed[...] = jnp.zeros(summed.shape, F32)
    planes_ref[...] = jnp.zeros(planes_ref.shape, F32)
    for q in range(4):
        lanes = slice(QUAD * q, QUAD * (q + 1))
        terms = plane_terms(fields, partners, sides, q, weights)
        for s in range(SLOTS):
            field = fields[s][:, lanes]
            start = field.astype(F32)
            value = start + rates2 * (terms[ROWS * s : ROWS * (s + 1)] + mm(rows_z, field))
            half_ref[s, :, lanes] = value.astype(BF16)
            if q == 0:
                edges_ref[s, :, :LANES] = value[:, :LANES]
            if q == 3:
                edges_ref[s, :, LANES:] = value[:, LANES:]
            both = value + start
            for h in range(2):
                part = slice(LANES * h, LANES * (h + 1))
                at = slice(QUAD * q + LANES * h, QUAD * q + LANES * (h + 1))
                split[2 * h] = value[:, part]
                split[2 * h + 1] = both[:, part]
                for p in range(2):
                    first = (EDGE - 1) * p
                    planes_ref[s, 8 * p : 8 * p + COMPS, at] = split[2 * h, pl.ds(first, COMPS, stride=EDGE), :]
                    row = PLANES * (2 * q + h) + 8 * p
                    summed[row : row + COMPS, LANES * s : LANES * (s + 1)] = (
                        split[2 * h + 1, pl.ds(first, COMPS, stride=EDGE), :]
                    )
    cells = mm(summed[...].astype(BF16), place_ref[...])
    for k in range(8):
        part = cells[PLANES * k : PLANES * (k + 1)]
        flux[pl.ds(2 * k, PLANES, stride=HALF), :] = part[:, :LANES]
        flux[pl.ds(2 * k + 1, PLANES, stride=HALF), :] = part[:, LANES:]
    cover = jnp.minimum(mm(jnp.ones((HALF, LANES), BF16), tables.to_coarse(None)), 1.0)
    coarse_rates = tables.rates(CROWS, HALF)
    for p in range(2):
        near = coarse_planes(coarse_ref, ((HALF - 1) * p,)).astype(F32)
        total = 0.25 * coarse_rates * flux[8 * HALF * p : 8 * HALF * p + CROWS, :]
        flux_ref[CROWS * p : CROWS * (p + 1), :] = total - coarse_rates * near * cover[:1]


def z_message_kernel(col, cnt, nbr, rate, coarse_ref, flux_in, y_near, y_far, near_ref, far_ref, arrived, flux):
    tables = Tables(col, cnt, nbr, rate)
    sort_arrivals("fine", y_near, y_far, arrived)
    flux[...] = flux_in[...]
    fine_pick, coarse_pick = plane_rows(EDGE, False), plane_rows(HALF, False)
    place = tables.to_coarse(None)
    rates = chain(iota((PLANES, LANES), 0) % 8, tables.rate + [jnp.zeros((), F32)] * 3)
    corners = []
    for k, face in ((0, 2), (1, 3)):
        row = mm(fine_pick, arrived[k, Y_ROW : Y_ROW + ROWS, :]).astype(BF16)
        corner = mm(coarse_pick, arrived[k, Y_NEAR : Y_NEAR + CROWS, :]).astype(BF16)
        corners.append(corner)
        ghost = mm(
            jnp.concatenate([row, corner], axis=1),
            jnp.concatenate([tables.linked_lanes(face), tables.from_coarse(face, True)], axis=0),
        )
        gain = (0.5 * rates * rates) * mm(ghost.astype(BF16), place)
        for p in range(2):
            at = pl.ds(CROWS * p + (HALF - 1) * k, COMPS, stride=HALF)
            flux[at, :] = flux[at, :] + gain[8 * p : 8 * p + COMPS]
    cover = jnp.minimum(mm(jnp.ones((HALF, LANES), BF16), place), 1.0).astype(BF16)
    messages = []
    for top in (True, False):
        near, following = (HALF - 1, HALF - 2) if top else (0, 1)
        messages.append(
            (
                (Z_NEAR, coarse_planes(coarse_ref, (near,))),
                (Z_NEXT, coarse_planes(coarse_ref, (following,))),
                (Z_FLUX, flux[CROWS * top : CROWS * (top + 1), :].astype(BF16)),
                (Z_LOW, corners[0]),
                (Z_HIGH, corners[1]),
                (Z_COVER, cover),
            )
        )
    store_by_parity("own", near_ref, far_ref, *messages)


SPAN = 32
DEEP = HALF + 2


def at_cell(c, z, y):
    return (c * DEEP + z + 1) * SPAN + 8 + y


def mixed(centre, total, r):
    total = total + pltpu.roll(centre, 1, 1) + pltpu.roll(centre, LANES - 1, 1)
    return centre + (0.5 * r) * (total - 6.0 * centre)


def own_mean(old, mean, tables, zs):
    for c in range(COMPS):
        for z in zs:
            total = (
                old[pl.ds(at_cell(c, z, -1), HALF), :]
                + old[pl.ds(at_cell(c, z, 1), HALF), :]
                + old[pl.ds(at_cell(c, z - 1, 0), HALF), :]
                + old[pl.ds(at_cell(c, z + 1, 0), HALF), :]
            )
            mean[pl.ds(at_cell(c, z, 0), HALF), :] = mixed(
                old[pl.ds(at_cell(c, z, 0), HALF), :], total, tables.rate[c]
            )


def strip_mean(old, mean, y_arr, tables):
    for c in range(COMPS):
        for k, y, inside in ((0, -1, 0), (1, HALF, HALF - 1)):
            at = Y_NEXT + c * HALF
            total = (
                y_arr[k, at : at + HALF, :].astype(F32)
                + old[pl.ds(at_cell(c, 0, inside), HALF, stride=SPAN), :]
                + old[pl.ds(at_cell(c, -1, y), HALF, stride=SPAN), :]
                + old[pl.ds(at_cell(c, 1, y), HALF, stride=SPAN), :]
            )
            mean[pl.ds(at_cell(c, 0, y), HALF, stride=SPAN), :] = mixed(
                old[pl.ds(at_cell(c, 0, y), HALF, stride=SPAN), :], total, tables.rate[c]
            )


def fill_old(old, coarse_ref, y_arr, zs):
    for c in range(COMPS):
        for z in zs:
            old[pl.ds(at_cell(c, z, 0), HALF), :] = coarse_ref[pl.ds((c * HALF + z) * HALF, HALF), :].astype(F32)
        for k, y in ((0, -1), (1, HALF)):
            at = Y_NEAR + c * HALF
            old[pl.ds(at_cell(c, 0, y), HALF, stride=SPAN), :] = y_arr[k, at : at + HALF, :].astype(F32)


def neighbour_rows(fine_ref, k):
    m, n = iota((SLOTS * LANES, LANES), 0), iota((SLOTS * LANES, LANES), 1)
    edge = LANES - EDGE if k else 0
    pack = ones_at((m // LANES == n // EDGE) & (m % LANES == n % EDGE + edge))
    tile = PLANE - LANES if k else 0
    return mm(jnp.concatenate([fine_ref[s, :, tile : tile + LANES] for s in range(SLOTS)], axis=1), pack)


class CoarseLanes:
    def __init__(self, tables, y_arr):
        x = iota((HALF, LANES), 1)
        covered, left, right = x < 0, x < 0, x < 0
        for s in range(SLOTS):
            x0, used = tables.start[s], tables.used[s] > 0
            covered = covered | ((x >= x0) & (x < x0 + HALF) & used)
            left = left | ((x == (x0 - 1) % LANES) & used & (tables.near[0][s] < 0))
            right = right | ((x == (x0 + HALF) % LANES) & used & (tables.near[1][s] < 0))
        self.covered = covered
        self.left, self.right = jnp.where(left, 1.0, 0.0), jnp.where(right, 1.0, 0.0)
        self.sides = self.left + self.right
        self.beside = [y_arr[k, Y_COVER : Y_COVER + HALF, :].astype(F32)[:1] for k in (0, 1)]

    def update(self, r, level0, level1, average, change):
        low, high = pltpu.roll(level0, LANES - 1, 1), pltpu.roll(level0, 1, 1)
        change = change - r * (self.sides * level1 + self.left * low + self.right * high)
        return jnp.where(self.covered, 0.125 * average, 2.0 * level1 - level0 + change).astype(BF16)

    def beyond_y(self, k, r, level0, level1, flux, corner):
        gain = (2.0 * r * r) * level0 - r * level1
        if corner is not None:
            gain = gain + (r * r) * corner
        return flux + self.beside[k] * gain


def early_kernel(*refs):
    ins, outs, scratch = refs[:14], refs[14:19], refs[19:]

    @pl.when(lax.axis_index("own") == 0)
    def _():
        middle_fine(*ins, *outs, *scratch)


def late_kernel(*refs):
    ins, done, coarse_out, faces_ref, outs, scratch = refs[:14], refs[14:19], refs[19], refs[20], refs[21:25], refs[25:]
    pairs, strips, y_arr, old, mean, split, average, outside = scratch
    is_early = lax.axis_index("own") == 0

    @pl.when(jnp.logical_not(is_early))
    def _():
        middle_fine(*ins, *outs, pairs, strips, y_arr, old, mean, split)

    @pl.when(is_early)
    def _():
        for source, target in zip(done, (*outs, pairs)):
            target[...] = source[...]
        levels(Tables(*ins[:4]), ins[5], ins[6], ins[7], y_arr, old, mean)

    middle_coarse(Tables(*ins[:4]), ins[13], pairs, y_arr, old, mean, average, outside, coarse_out, faces_ref)


def levels(tables, coarse_ref, y_near, y_far, y_arr, old, mean):
    sort_arrivals("fine", y_near, y_far, y_arr)
    fill_old(old, coarse_ref, y_arr, range(HALF))
    for c in range(COMPS):
        for z in (-1, HALF):
            old[pl.ds(at_cell(c, z, 0) - 8, SPAN), :] = jnp.zeros((SPAN, LANES), F32)
    own_mean(old, mean, tables, range(HALF))
    strip_mean(old, mean, y_arr, tables)


def middle_fine(
    col, cnt, nbr, rate, fine_ref, coarse_ref, y_near, y_far, half_in, edges_ref, planes_in, weights, side_sum, place_ref,
    fine_out, rows_ref, planes_ref, theirs_ref, pairs, strips, y_arr, old, mean, split,
):
    tables = Tables(col, cnt, nbr, rate)
    levels(tables, coarse_ref, y_near, y_far, y_arr, old, mean)
    rates = tables.rates(ROWS, EDGE)
    rates2 = 2.0 * jnp.concatenate([rates, rates], axis=1)
    double, rows_z = copies(ROWS, 2), z_stencil()
    cells = jnp.concatenate(
        [mean[pl.ds(at_cell(c, z, 0), HALF), :] for c in range(COMPS) for z in range(HALF)], axis=0
    ).astype(BF16)
    m, n = iota((CELLS, LANES), 0), iota((CELLS, LANES), 1)
    picked = jnp.where(m % HALF == n % HALF, mm(cells, tables.side_pick()), 0.0).astype(BF16)
    sides = [part.astype(BF16) for part in slot_sides(mm(side_sum[...], picked))]

    def level_row(level, y):
        rows = [level[pl.ds(at_cell(c, 0, y), HALF, stride=SPAN), :] for c in range(COMPS)]
        return mm(double, jnp.concatenate(rows, axis=0).astype(BF16)).astype(BF16)

    planes_ref[...] = planes_in[...]

    def half(t):
        return jnp.concatenate([strips[t, :, :LANES], half_in[t, :, LANES : PLANE - LANES], strips[t, :, LANES:]], axis=1)

    second = []
    plane_rates = chain(iota((PLANES, LANES), 0) % 8, tables.rate + [jnp.zeros((), F32)] * 3)
    for k, y in ((0, -1), (1, HALF)):
        linked, opened = tables.linked_lanes(2 + k), tables.from_coarse(2 + k, True)
        row = y_arr[k, Y_ROW : Y_ROW + ROWS, :]
        ghost = mm(jnp.concatenate([row, level_row(old, y)], axis=1), jnp.concatenate([linked, opened], axis=0))
        plane_ghost = mm(plane_rows(EDGE, False), ghost.astype(BF16))
        tile = slice(PLANE - LANES, PLANE) if k else slice(0, LANES)
        part = slice(LANES * k, LANES * (k + 1))
        for s in range(SLOTS):
            add = edge_lanes(ghost, s, bool(k))[:, part]
            strips[s, :, part] = (edges_ref[s, :, part] + 2.0 * rates * add).astype(BF16)
            add = edge_lanes(plane_ghost, s, bool(k))[:, part]
            planes_ref[s, :, tile] = planes_ref[s, :, tile] + 2.0 * plane_rates * add
        theirs = mm(y_arr[k, Y_HALF : Y_HALF + ROWS, :], linked) + 2.0 * rates * neighbour_rows(fine_ref, k)
        theirs_ref[k] = theirs
        theirs = theirs.astype(BF16).astype(F32)
        is_linked = chain(iota((ROWS, LANES), 1) // EDGE, tables.near[2 + k]) >= 0
        second.append(jnp.where(is_linked, theirs, mm(level_row(mean, y), opened)))

    rows_ref[...] = jnp.zeros(rows_ref.shape, F32)
    fields = [half(s) for s in range(SLOTS)]
    partners = partner_columns(half, tables, ROWS)
    for q in range(4):
        lanes = slice(QUAD * q, QUAD * (q + 1))
        terms = plane_terms(fields, partners, sides, q, weights)
        for s in range(SLOTS):
            field = fields[s][:, lanes]
            around = terms[ROWS * s : ROWS * (s + 1)] + mm(rows_z, field)
            if q == 0:
                around = around + edge_lanes(second[0], s, False)
            if q == 3:
                around = around + edge_lanes(second[1], s, True)
            start = field.astype(F32)
            for h in range(2):
                split[h, :ROWS, :] = start[:, LANES * h : LANES * (h + 1)]
                split[h, ROWS : 2 * ROWS, :] = (
                    split[h, :ROWS, :] + fine_ref[s, :, QUAD * q + LANES * h : QUAD * q + LANES * (h + 1)].astype(F32)
                )
                pairs[0, 2 * q + h, :, LANES * s : LANES * (s + 1)] = (
                    split[h, pl.ds(ROWS, CROWS, stride=2), :] + split[h, pl.ds(ROWS + 1, CROWS, stride=2), :]
                ).astype(BF16)
                at = slice(QUAD * q + LANES * h, QUAD * q + LANES * (h + 1))
                for w, first in enumerate((1, 2, EDGE - 3, EDGE - 2)):
                    rows_ref[s, 8 * w : 8 * w + COMPS, at] = split[h, pl.ds(first, COMPS, stride=EDGE), :]
            value = jnp.where(tables.used[s] > 0, start + rates2 * around, 0.0).astype(BF16)
            fine_out[s, :, lanes] = value
            value = value.astype(F32)
            for h in range(2):
                split[h, 2 * ROWS : 3 * ROWS, :] = value[:, LANES * h : LANES * (h + 1)]
                pairs[1, 2 * q + h, :, LANES * s : LANES * (s + 1)] = (
                    split[h, pl.ds(2 * ROWS, CROWS, stride=2), :] + split[h, pl.ds(2 * ROWS + 1, CROWS, stride=2), :]
                ).astype(BF16)


def middle_coarse(tables, place_ref, pairs, y_arr, old, mean, average, outside, coarse_out, faces_ref):
    faces = mm(pairs[0].reshape(8 * CROWS, SLOTS * LANES), tables.pool_spread(1))
    cells = mm(pairs[1].reshape(8 * CROWS, SLOTS * LANES), place_ref[...])
    coarse_rates = tables.rates(CROWS, HALF)
    scale = 0.25 * coarse_rates
    for j in range(2):
        lanes = slice(LANES * j, LANES * (j + 1))
        for k in range(8):
            at = pl.ds(2 * k + j, CROWS, stride=HALF)
            outside[at, :] = scale * faces[CROWS * k : CROWS * (k + 1), lanes]
            average[at, :] = cells[CROWS * k : CROWS * (k + 1), lanes]
    for c in range(COMPS):
        for p in range(2):
            at = CROWS * p + HALF * c
            faces_ref[at : at + HALF, :] = outside[pl.ds((c * HALF + (HALF - 1) * p) * HALF, HALF), :]

    masks = CoarseLanes(tables, y_arr)

    def strip(level, y):
        return jnp.concatenate([level[pl.ds(at_cell(c, 0, y), HALF, stride=SPAN), :] for c in range(COMPS)], axis=0)

    for k, y in ((0, 0), (1, HALF - 1)):
        at = pl.ds(y, CROWS, stride=HALF)
        flux = y_arr[k, Y_FLUX : Y_FLUX + CROWS, :].astype(F32)
        outside[at, :] = outside[at, :] + masks.beyond_y(k, coarse_rates, strip(old, y), strip(mean, y), flux, None)
    for c in range(COMPS):
        for z in range(HALF):
            line = pl.ds((c * HALF + z) * HALF, HALF)
            if z in (0, HALF - 1):
                coarse_out[line, :] = jnp.zeros((HALF, LANES), BF16)
                continue
            coarse_out[line, :] = masks.update(
                tables.rate[c], old[pl.ds(at_cell(c, z, 0), HALF), :], mean[pl.ds(at_cell(c, z, 0), HALF), :],
                average[line, :], outside[line, :],
            )


NEAR = 32


def last_kernel(
    col, cnt, nbr, rate, coarse_ref, y_near, y_far, z_near, z_far, weights, place_ref,
    coarse_in, fine_in, rows_ref, planes_ref, theirs_ref, faces_ref,
    coarse_out, fine_hbm, y_arr, z_arr, old, mean, near, split, following, spread, ghost, level_rows, put, fine_out, sems,
):
    tables = Tables(col, cnt, nbr, rate)
    sort_arrivals("fine", y_near, y_far, y_arr)
    sort_arrivals("own", z_near, z_far, z_arr)
    fill_old(old, coarse_ref, y_arr, (0, 1, HALF - 2, HALF - 1))
    for k in (0, 1):
        following[k] = y_arr[k, Y_NEXT : Y_NEXT + CROWS, :].astype(F32)
    for c in range(COMPS):
        for k, z in ((0, -1), (1, HALF)):
            at = Z_NEAR + c * HALF
            old[pl.ds(at_cell(c, z, 0), HALF), :] = z_arr[k, at : at + HALF, :].astype(F32)
    by_comp = DEEP * SPAN
    for k, z in ((0, -1), (1, HALF)):
        first = 0 if k else 8
        low = z_arr[k, Z_LOW : Z_LOW + HALF, :].astype(F32)
        high = z_arr[k, Z_HIGH : Z_HIGH + HALF, :].astype(F32)
        old[pl.ds(at_cell(0, z, -1), COMPS, stride=by_comp), :] = low[first : first + COMPS]
        old[pl.ds(at_cell(0, z, HALF), COMPS, stride=by_comp), :] = high[first : first + COMPS]
    own_mean(old, mean, tables, (0, HALF - 1))
    comp_rates = chain(iota((COMPS, LANES), 0), tables.rate)
    level_rows[...] = jnp.zeros(level_rows.shape, F32)
    for k, y, inside in ((0, -1, 0), (1, HALF, HALF - 1)):
        for p, z in ((0, 0), (1, HALF - 1)):
            total = (
                following[k, pl.ds(z, COMPS, stride=HALF), :]
                + old[pl.ds(at_cell(0, z, inside), COMPS, stride=by_comp), :]
                + old[pl.ds(at_cell(0, z - 1, y), COMPS, stride=by_comp), :]
                + old[pl.ds(at_cell(0, z + 1, y), COMPS, stride=by_comp), :]
            )
            value = mixed(old[pl.ds(at_cell(0, z, y), COMPS, stride=by_comp), :], total, comp_rates)
            for w in (2 * p, 2 * p + 1):
                level_rows[k, 8 * w : 8 * w + COMPS, :] = value
    for c in range(COMPS):
        for k, z, inside in ((0, -1, 0), (1, HALF, HALF - 1)):
            at = Z_NEXT + c * HALF
            total = (
                z_arr[k, at : at + HALF, :].astype(F32)
                + old[pl.ds(at_cell(c, inside, 0), HALF), :]
                + old[pl.ds(at_cell(c, z, -1), HALF), :]
                + old[pl.ds(at_cell(c, z, 1), HALF), :]
            )
            mean[pl.ds(at_cell(c, z, 0), HALF), :] = mixed(
                old[pl.ds(at_cell(c, z, 0), HALF), :], total, tables.rate[c]
            )

    window = tables.from_coarse(None, False)
    n = iota((2 * CROWS, LANES), 1)

    def planes_of(level, zs):
        return jnp.concatenate([level[pl.ds(at_cell(c, z, 0), HALF), :] for z in zs for c in range(COMPS)], axis=0)

    first_y = iota((COMPS, LANES), 1) < 2 * EDGE

    def ghost_rows(level, i):
        planes = mm(planes_of(level, (-1, HALF)).astype(BF16), window)
        for s in range(SLOTS):
            part = jnp.where(n // EDGE == s, planes, 0.0)
            part = part + pltpu.roll(part, EDGE, 1)
            spread[s] = part + pltpu.roll(part, 2 * EDGE, 1)
            for k in range(8):
                for p in range(2):
                    even = spread[s, pl.ds(CROWS * p + 2 * k, COMPS, stride=HALF), :]
                    odd = spread[s, pl.ds(CROWS * p + 2 * k + 1, COMPS, stride=HALF), :]
                    ghost[i, s, 8 * p : 8 * p + COMPS, LANES * k : LANES * (k + 1)] = jnp.where(first_y, even, odd)

    ghost[...] = jnp.zeros(ghost.shape, F32)
    ghost_rows(old, 0)
    ghost_rows(mean, 1)
    rates = chain(iota((NEAR, LANES), 0) % 8, tables.rate + [jnp.zeros((), F32)] * 3)
    rates2 = 2.0 * jnp.concatenate([rates, rates], axis=1)
    wide = 2.0 * chain(iota((2 * 8, PLANE), 0) % 8, tables.rate + [jnp.zeros((), F32)] * 3)

    along = []
    for s in range(SLOTS):
        ends = (planes_ref[s] + wide * ghost[0, s]).astype(BF16).astype(F32)
        one, two, next_last, last = (rows_ref[s, 8 * w : 8 * (w + 1), :] for w in range(4))
        near[s] = jnp.concatenate([ends[:8], one, last, ends[8:]], axis=0).astype(BF16)
        along.append(
            jnp.concatenate(
                [
                    one - 6.0 * ends[:8] + ghost[1, s, :8],
                    ends[:8] + two - 6.0 * one,
                    ends[8:] + next_last - 6.0 * last,
                    last - 6.0 * ends[8:] + ghost[1, s, 8:],
                ],
                axis=0,
            )
        )

    m = iota((2 * CROWS, LANES), 0)
    picked = jnp.where(
        m % HALF == n % HALF, mm(planes_of(mean, (0, HALF - 1)).astype(BF16), tables.side_pick()), 0.0
    ).astype(BF16)
    out, src = iota((NEAR, 2 * CROWS), 0), iota((NEAR, 2 * CROWS), 1)
    side_sum = ones_at((out % 8 == src % CROWS // HALF) & (out % 8 < COMPS) & (out // 16 == src // CROWS))
    sides = [part.astype(BF16) for part in slot_sides(mm(side_sum, picked))]
    ghosts = []
    zero = jnp.zeros((8, LANES), F32)
    for k in (0, 1):
        at = Z_HIGH if k else Z_LOW
        corner = jnp.concatenate([z_arr[0, at : at + PLANES, :], z_arr[1, at : at + PLANES, :]], axis=0)
        corner = mm(corner, window)
        for w, first in enumerate((0, 1, EDGE - 2, EDGE - 1)):
            level_rows[2, 8 * w : 8 * w + COMPS, :] = theirs_ref[k, pl.ds(first, COMPS, stride=EDGE), :]
        theirs = level_rows[2] + 2.0 * rates * jnp.concatenate([corner[8:16], zero, zero, corner[16:24]], axis=0)
        theirs = theirs.astype(BF16).astype(F32)
        is_linked = chain(iota((NEAR, LANES), 1) // EDGE, tables.near[2 + k]) >= 0
        level = mm(level_rows[k].astype(BF16), tables.from_coarse(2 + k, True))
        ghosts.append(jnp.where(is_linked, theirs, level))
    fields = [near[s] for s in range(SLOTS)]
    partners = partner_columns(lambda t: near[t], tables, NEAR)
    fresh = []
    for q in range(4):
        lanes = slice(QUAD * q, QUAD * (q + 1))
        terms = plane_terms(fields, partners, sides, q, weights)
        for s in range(SLOTS):
            field = fields[s][:, lanes]
            around = terms[NEAR * s : NEAR * (s + 1)] + along[s][:, lanes]
            if q == 0:
                around = around + edge_lanes(ghosts[0], s, False)
            if q == 3:
                around = around + edge_lanes(ghosts[1], s, True)
            value = jnp.where(tables.used[s] > 0, field.astype(F32) + rates2 * around, 0.0).astype(BF16)
            fresh.append(value)
            value = value.astype(F32)
            for h in range(2):
                for w, first in enumerate((0, 1, EDGE - 2, EDGE - 1)):
                    put[s, 2 * q + h, pl.ds(first, COMPS, stride=EDGE), :] = (
                        value[8 * w : 8 * w + COMPS, LANES * h : LANES * (h + 1)]
                    )
    a = iota((ROWS, LANES), 0) % EDGE
    replaced = (a < 2) | (a >= EDGE - 2)
    sends = []
    for s in range(SLOTS):
        for k in range(8):
            lanes = slice(LANES * k, LANES * (k + 1))
            fine_out[s, :, lanes] = jnp.where(replaced, put[s, k], fine_in[s, :, lanes].astype(F32)).astype(BF16)
        sends.append(pltpu.make_async_copy(fine_out.at[s], fine_hbm.at[s], sems.at[s]))
        sends[s].start()

    tall = jnp.concatenate(
        [
            jnp.concatenate([fresh[SLOTS * q + s][:, LANES * h : LANES * (h + 1)] for s in range(SLOTS)], axis=1)
            for q in range(4)
            for h in range(2)
        ],
        axis=0,
    )
    cells = mm(tall, place_ref[...])
    for k in range(8):
        part = cells[NEAR * k : NEAR * (k + 1)]
        for j in range(2):
            lane = slice(LANES * j, LANES * (j + 1))
            for p in range(2):
                pair = part[16 * p : 16 * p + 8, lane] + part[16 * p + 8 : 16 * p + 16, lane]
                split[pl.ds(8 * HALF * p + 2 * k + j, 8, stride=HALF), :] = pair

    coarse_out[...] = coarse_in[...]
    masks = CoarseLanes(tables, y_arr)
    row = iota((HALF, LANES), 0)
    for c in range(COMPS):
        r = tables.rate[c]
        y_flux = [y_arr[k, Y_FLUX + c * HALF : Y_FLUX + (c + 1) * HALF, :].astype(F32) for k in (0, 1)]
        for p, z in ((0, 0), (1, HALF - 1)):
            beyond = -1 if z == 0 else HALF
            level0, level1 = old[pl.ds(at_cell(c, z, 0), HALF), :], mean[pl.ds(at_cell(c, z, 0), HALF), :]
            halo = old[pl.ds(at_cell(c, beyond, 0), HALF), :]
            halo = masks.left * pltpu.roll(halo, LANES - 1, 1) + masks.right * pltpu.roll(halo, 1, 1)
            at = CROWS * p + HALF * c
            change = faces_ref[at : at + HALF, :] + (r * r) * halo
            for k, y in ((0, 0), (1, HALF - 1)):
                corner = old[pl.ds(at_cell(c, beyond, HALF if k else -1), 1), :]
                extra = masks.beyond_y(k, r, level0[y : y + 1], level1[y : y + 1], y_flux[k][z : z + 1], corner)
                change = change + jnp.where(row == y, extra, 0.0)
            flux = z_arr[p, Z_FLUX + c * HALF : Z_FLUX + (c + 1) * HALF, :].astype(F32)
            ahead = z_arr[p, Z_COVER : Z_COVER + HALF, :].astype(F32)
            change = change + flux + ahead * ((2.0 * r * r) * level0 - r * level1)
            coarse_out[pl.ds((c * HALF + z) * HALF, HALF), :] = masks.update(
                r, level0, level1, split[pl.ds(8 * HALF * p + c * HALF, HALF), :], change
            )
    for send in sends:
        send.wait()


SCALARS = [pl.BlockSpec(memory_space=pltpu.SMEM)] * 4
PARAMS = pltpu.CompilerParams(vmem_limit_bytes=32 * 1024 * 1024)
FETCH_PARAMS = pltpu.CompilerParams(vmem_limit_bytes=60 * 1024 * 1024)


def whole():
    return pl.BlockSpec(memory_space=pltpu.VMEM)


def local(coarse_cells, fine_cells, diffusivity, patch_column, patch_count, neighbor_slot):
    fine = fine_cells.reshape(SLOTS, ROWS, PLANE)
    coarse = coarse_cells.reshape(CELLS, LANES)
    tables = (patch_column, patch_count, neighbor_slot, diffusivity)
    n_own, n_fine = lax.axis_size("own"), lax.axis_size("fine")

    def swap(value, axis, count, far):
        shift = 1 if far else 0
        pairs = []
        for i in range(count):
            partner = ((i - shift) ^ 1) + shift
            pairs.append((i, partner % count))
        return lax.ppermute(value, axis, pairs)

    y_shape = jax.ShapeDtypeStruct((Y_ROWS, LANES), BF16)
    field_shape = jax.ShapeDtypeStruct((SLOTS, ROWS, PLANE), BF16)
    cells_shape = jax.ShapeDtypeStruct((CELLS, LANES), BF16)
    y_near, y_far = pl.pallas_call(
        y_message_kernel,
        in_specs=[pl.BlockSpec(memory_space=pl.ANY)] * 6,
        out_specs=[whole()] * 2,
        out_shape=[y_shape] * 2,
        scratch_shapes=[
            pltpu.SMEM((SLOTS,), jnp.int32),
            pltpu.SMEM((1,), jnp.int32),
            pltpu.SMEM((SLOTS, 4), jnp.int32),
            pltpu.SMEM((COMPS,), F32),
            pltpu.VMEM((SLOTS, ROWS, LANES), BF16),
            pltpu.VMEM((SLOTS, ROWS, LANES), BF16),
            pltpu.VMEM((CELLS, LANES), BF16),
            pltpu.VMEM((CELLS, LANES), F32),
            pltpu.VMEM((2, SLOTS * LANES, QUAD), BF16),
            pltpu.VMEM((ROWS, ROWS), BF16),
            pltpu.SemaphoreType.DMA((7,)),
        ],
        compiler_params=FETCH_PARAMS,
        name="y_messages",
    )(*tables, fine, coarse)
    y_near, y_far = swap(y_near, "fine", n_fine, False), swap(y_far, "fine", n_fine, True)

    planes_shape = jax.ShapeDtypeStruct((SLOTS, PLANES, PLANE), F32)
    level = pltpu.VMEM((COMPS * DEEP * SPAN, LANES), F32)
    weights, side_sum = jnp.asarray(plane_weights()), jnp.asarray(side_rows())
    half, edges, planes, flux, place = pl.pallas_call(
        interior_kernel,
        in_specs=SCALARS + [whole()] * 4,
        out_specs=[whole()] * 5,
        out_shape=[
            field_shape,
            jax.ShapeDtypeStruct((SLOTS, ROWS, QUAD), F32),
            planes_shape,
            jax.ShapeDtypeStruct((2 * CROWS, LANES), F32),
            jax.ShapeDtypeStruct((SLOTS * LANES, QUAD), BF16),
        ],
        scratch_shapes=[
            pltpu.VMEM((PLANES * HALF, LANES), F32),
            pltpu.VMEM((8 * PLANES, SLOTS * LANES), F32),
            pltpu.VMEM((4, ROWS, LANES), F32),
        ],
        compiler_params=PARAMS,
        cost_estimate=pl.CostEstimate(flops=2_000_000_000, bytes_accessed=5_000_000, transcendentals=0),
        name="interior",
    )(*tables, fine, coarse, weights, side_sum)

    z_shape = jax.ShapeDtypeStruct((Z_ROWS, LANES), BF16)
    z_near, z_far = pl.pallas_call(
        z_message_kernel,
        in_specs=SCALARS + [whole()] * 4,
        out_specs=[whole()] * 2,
        out_shape=[z_shape] * 2,
        scratch_shapes=[pltpu.VMEM((2, Y_ROWS, LANES), BF16), pltpu.VMEM((2 * CROWS, LANES), F32)],
        compiler_params=PARAMS,
        name="z_messages",
    )(*tables, coarse, flux, y_near, y_far)
    fine_shapes = [
        field_shape,
        jax.ShapeDtypeStruct((SLOTS, 32, PLANE), F32),
        planes_shape,
        jax.ShapeDtypeStruct((2, ROWS, LANES), F32),
    ]
    pairs_shape = (2, 8, CROWS, SLOTS * LANES)
    middle_args = (*tables, fine, coarse, y_near, y_far, half, edges, planes, weights, side_sum, place)
    scratch = [
        pltpu.VMEM((SLOTS, ROWS, QUAD), BF16),
        pltpu.VMEM((2, Y_ROWS, LANES), BF16),
        level,
        level,
        pltpu.VMEM((2, 3 * ROWS, LANES), F32),
    ]
    z_near = swap(z_near, "own", n_own, False)
    done = pl.pallas_call(
        early_kernel,
        in_specs=SCALARS + [whole()] * 10,
        out_specs=[whole()] * 5,
        out_shape=fine_shapes + [jax.ShapeDtypeStruct(pairs_shape, BF16)],
        scratch_shapes=scratch,
        compiler_params=PARAMS,
        cost_estimate=pl.CostEstimate(flops=3_000_000_000, bytes_accessed=8_000_000, transcendentals=0),
        name="early",
    )(*middle_args)
    z_far, done = lax.optimization_barrier((z_far, done))
    z_far = swap(z_far, "own", n_own, True)
    coarse_part, faces, *parts = pl.pallas_call(
        late_kernel,
        in_specs=SCALARS + [whole()] * 15,
        out_specs=[whole()] * 6,
        out_shape=[cells_shape, jax.ShapeDtypeStruct((2 * CROWS, LANES), F32)] + fine_shapes,
        scratch_shapes=[
            pltpu.VMEM(pairs_shape, BF16),
            *scratch,
            pltpu.VMEM((CELLS, LANES), F32),
            pltpu.VMEM((CELLS, LANES), F32),
        ],
        compiler_params=PARAMS,
        cost_estimate=pl.CostEstimate(flops=3_000_000_000, bytes_accessed=8_000_000, transcendentals=0),
        name="late",
    )(*middle_args, *done)
    parts = (coarse_part, *parts, faces)

    coarse_new, fine_new = pl.pallas_call(
        last_kernel,
        in_specs=SCALARS + [whole()] * 13,
        out_specs=[whole(), pl.BlockSpec(memory_space=pl.ANY)],
        out_shape=[cells_shape, field_shape],
        scratch_shapes=[
            pltpu.VMEM((2, Y_ROWS, LANES), BF16),
            pltpu.VMEM((2, Z_ROWS, LANES), BF16),
            level,
            level,
            pltpu.VMEM((SLOTS, 32, PLANE), BF16),
            pltpu.VMEM((PLANES * HALF, LANES), F32),
            pltpu.VMEM((2, CROWS, LANES), F32),
            pltpu.VMEM((SLOTS, 2 * CROWS, LANES), F32),
            pltpu.VMEM((2, SLOTS, PLANES, PLANE), F32),
            pltpu.VMEM((3, 32, LANES), F32),
            pltpu.VMEM((SLOTS, 8, ROWS, LANES), F32),
            pltpu.VMEM((SLOTS, ROWS, PLANE), BF16),
            pltpu.SemaphoreType.DMA((SLOTS,)),
        ],
        compiler_params=PARAMS,
        name="last",
    )(*tables, coarse, y_near, y_far, z_near, z_far, weights, place, *parts)
    return coarse_new.reshape(coarse_cells.shape), fine_new.reshape(fine_cells.shape)


def solution(mesh):
    return jax.shard_map(
        local,
        mesh=mesh,
        in_specs=(
            P(None, "own", "fine", None),
            P(("own", "fine"), None, None, None),
            P(),
            P(("own", "fine")),
            P(("own", "fine")),
            P(("own", "fine"), None),
        ),
        out_specs=(P(None, "own", "fine", None), P(("own", "fine"), None, None, None)),
        check_vma=False,
    )
```

```python
import functools

import jax
import jax.numpy as jnp
import numpy as np
from jax import lax
from jax.experimental import pallas as pl
from jax.experimental.pallas import tpu as pltpu
from jax.sharding import PartitionSpec as P

F32, BF16 = jnp.float32, jnp.bfloat16
SLOTS, COMPS, EDGE, HALF, LANES = 4, 5, 32, 16, 128
ROWS = COMPS * EDGE
CROWS = COMPS * HALF
CELLS = CROWS * HALF
PLANE = EDGE * EDGE
QUAD = 256

Y_NEAR, Y_NEXT, Y_ROW, Y_HALF, Y_FLUX, Y_COVER = 0, 80, 160, 320, 480, 560
Y_ROWS = 576
Z_NEAR, Z_NEXT, Z_FLUX, Z_LOW, Z_HIGH, Z_COVER = 0, 80, 160, 240, 256, 272
Z_ROWS = 288


def iota(shape, dim):
    return lax.broadcasted_iota(jnp.int32, shape, dim)


def ones_at(mask):
    return jnp.where(mask, 1.0, 0.0).astype(BF16)


def mm(left, right):
    return lax.dot_general(left, right, (((1,), (0,)), ((), ())), preferred_element_type=F32)


def chain(index, values):
    out = jnp.full(index.shape, values[-1], values[-1].dtype)
    for k in range(len(values) - 2, -1, -1):
        out = jnp.where(index == k, values[k], out)
    return out


class Tables:
    def __init__(self, col, cnt, nbr, rate):
        self.start = [col[s] * HALF for s in range(SLOTS)]
        self.used = [jnp.where(s < cnt[0], 1, 0) for s in range(SLOTS)]
        self.near = [[nbr[s, f] for s in range(SLOTS)] for f in range(4)]
        self.rate = [rate[c] for c in range(COMPS)]

    def rates(self, rows, per):
        return chain(iota((rows, LANES), 0) // per, self.rate)

    def packed(self, dim):
        n, x = iota((LANES, LANES), dim), iota((LANES, LANES), 1 - dim)
        return n // EDGE, n % EDGE, x

    def to_coarse(self, face):
        s, e, x = self.packed(0)
        hit = (x == chain(s, self.start) + e // 2) & (chain(s, self.used) > 0)
        if face is not None:
            hit = hit & (chain(s, self.near[face]) < 0)
        return ones_at(hit)

    def from_coarse(self, face, unlinked):
        s, e, x = self.packed(1)
        hit = x == chain(s, self.start) + e // 2
        if unlinked:
            hit = hit & (chain(s, self.near[face]) < 0)
        return ones_at(hit)

    def linked_lanes(self, face):
        s, e, n = self.packed(1)
        return ones_at(n == chain(s, self.near[face]) * EDGE + jnp.where(chain(s, self.near[face]) < 0, -LANES, e))

    def row_stencil(self):
        s, e, n = self.packed(1)
        low, high, x0 = chain(s, self.near[0]), chain(s, self.near[1]), chain(s, self.start)
        inside = (n // EDGE == s) & ((n % EDGE == e - 1) | (n % EDGE == e + 1))
        at_low = (e == 0) & (low >= 0) & (n == low * EDGE + EDGE - 1)
        at_high = (e == EDGE - 1) & (high >= 0) & (n == high * EDGE)
        left = (e == 0) & (low < 0) & (n == (x0 - 1) % LANES)
        right = (e == EDGE - 1) & (high < 0) & (n == (x0 + HALF) % LANES)
        return jnp.concatenate([ones_at(inside | at_low | at_high), ones_at(left | right)], axis=0)

    def side_pick(self):
        n, x = iota((LANES, LANES), 1), iota((LANES, LANES), 0)
        s, high = n // EDGE, n % EDGE >= HALF
        x0 = chain(s, self.start)
        spot = jnp.where(high, (x0 + HALF) % LANES, (x0 - 1) % LANES)
        open_face = jnp.where(high, chain(s, self.near[1]), chain(s, self.near[0])) < 0
        return ones_at((x == spot) & open_face)

    def pool_spread(self, mode):
        m, x = iota((SLOTS * LANES, LANES), 0), iota((SLOTS * LANES, LANES), 1)
        s, lane = m // LANES, m % LANES
        e, x0 = lane % EDGE, chain(s, self.start)
        if mode == 0:
            target = jnp.where(chain(s, self.used) > 0, x0 + e // 2, -1)
        else:
            low = [jnp.where((self.used[k] > 0) & (self.near[0][k] < 0), (self.start[k] - 1) % LANES, -1) for k in range(SLOTS)]
            high = [jnp.where((self.used[k] > 0) & (self.near[1][k] < 0), (self.start[k] + HALF) % LANES, -1) for k in range(SLOTS)]
            target = jnp.where(e == 0, chain(s, low), jnp.where(e == EDGE - 1, chain(s, high), -1))
        first = lane < 2 * EDGE
        hit = x == target
        return jnp.concatenate([ones_at(hit & first), ones_at(hit & jnp.logical_not(first))], axis=1)


def copies(rows, per):
    out, src = iota((rows, rows // per), 0), iota((rows, rows // per), 1)
    return ones_at(out // per == src)


def pair_rows():
    out, src = iota((CROWS, ROWS), 0), iota((CROWS, ROWS), 1)
    return ones_at(src // 2 == out)


def z_stencil():
    out, src = iota((ROWS, ROWS), 0), iota((ROWS, ROWS), 1)
    same = out // EDGE == src // EDGE
    beside = same & ((src == out + 1) | (src == out - 1))
    return jnp.where(src == out, -6.0, jnp.where(beside, 1.0, 0.0)).astype(BF16)


def grid_of(rows, columns):
    return np.indices((rows, columns))


def plane_stencil():
    m, n = grid_of(3 * QUAD, QUAD)
    e = n % EDGE
    own = (m < QUAD) & (
        ((m == n - 1) & (e > 0)) | ((m == n + 1) & (e < EDGE - 1)) | (m == n - EDGE) | (m == n + EDGE)
    )
    before = (m >= QUAD) & (m < QUAD + LANES) & (m - QUAD - LANES == n - EDGE)
    after = (m >= QUAD + LANES) & (m < 2 * QUAD) & (m - QUAD - LANES + QUAD == n + EDGE)
    p = m - 2 * QUAD
    partner = (m >= 2 * QUAD) & (
        ((e == 0) & (p == n + EDGE - 1)) | ((e == EDGE - 1) & (p == n - EDGE + 1))
    )
    return own | before | after | partner


def side_place(q):
    m, n = grid_of(LANES, QUAD)
    y, e = (n // EDGE + q * (QUAD // EDGE)) // 2, n % EDGE
    return (m < EDGE) & (m % HALF == y) & (e == np.where(m < HALF, 0, EDGE - 1))


def plane_weights():
    return np.concatenate([plane_stencil()] + [side_place(q) for q in range(4)]).astype(BF16)


def side_rows():
    out, src = grid_of(ROWS, CELLS)
    return (out // 2 == src // HALF).astype(BF16)


def partner_columns(load, tables, rows):
    lane = iota((rows, PLANE), 1) % EDGE
    at_low = jnp.where(lane == EDGE - 1, 1.0, 0.0).astype(BF16)
    at_high = jnp.where(lane == 0, 1.0, 0.0).astype(BF16)
    out = []
    for s in range(SLOTS):
        low, high = tables.near[0][s], tables.near[1][s]
        has_low = jnp.where(low >= 0, 1.0, 0.0).astype(BF16)
        has_high = jnp.where(high >= 0, 1.0, 0.0).astype(BF16)
        out.append(
            load(jnp.maximum(low, 0)) * (at_low * has_low) + load(jnp.maximum(high, 0)) * (at_high * has_high)
        )
    return out


def plane_terms(fields, partners, sides, q, weights):
    lo, hi = QUAD * q, QUAD * (q + 1)
    parts = []
    for s in range(SLOTS):
        field = fields[s]
        rows = field.shape[0]
        none = jnp.zeros((rows, LANES), BF16)
        parts.append(
            jnp.concatenate(
                [
                    field[:, lo:hi],
                    field[:, lo - LANES : lo] if q else none,
                    field[:, hi : hi + LANES] if q < 3 else none,
                    partners[s][:, lo:hi],
                    sides[s],
                ],
                axis=1,
            )
        )
    place = 3 * QUAD + LANES * q
    table = jnp.concatenate([weights[: 3 * QUAD, :], weights[place : place + LANES, :]], axis=0)
    return mm(jnp.concatenate(parts, axis=0), table)


def slot_sides(sides):
    return [sides if s == 0 else pltpu.roll(sides, LANES - EDGE * s, 1) for s in range(SLOTS)]


def edge_lanes(ghost, s, top):
    shift = (LANES - EDGE * (s + 1 if top else s)) % LANES
    moved = pltpu.roll(ghost, shift, 1) if shift else ghost
    lane = iota(ghost.shape, 1)
    kept = jnp.where(lane >= LANES - EDGE if top else lane < EDGE, moved, 0.0)
    none = jnp.zeros(ghost.shape, F32)
    return jnp.concatenate([none, kept] if top else [kept, none], axis=1)


def y_message_kernel(
    col_hbm, cnt_hbm, nbr_hbm, rate_hbm, fine_hbm, coarse_hbm, near_ref, far_ref,
    col, cnt, nbr, rate, low_ref, high_ref, coarse_ref, level, packs, rows_z, sems,
):
    fetches = [
        pltpu.make_async_copy(source, target, sems.at[i])
        for i, (source, target) in enumerate(
            (
                (col_hbm, col),
                (cnt_hbm, cnt),
                (nbr_hbm, nbr),
                (rate_hbm, rate),
                (coarse_hbm, coarse_ref),
                (fine_hbm.at[:, :, 0:LANES], low_ref),
                (fine_hbm.at[:, :, PLANE - LANES : PLANE], high_ref),
            )
        )
    ]
    for fetch in fetches:
        fetch.start()
    m, n = iota((SLOTS * LANES, QUAD), 0), iota((SLOTS * LANES, QUAD), 1)
    for i, (edge, inner) in enumerate(((0, EDGE), (LANES - EDGE, LANES - 2 * EDGE))):
        packs[i] = ones_at(
            (m // LANES == n % LANES // EDGE) & (m % LANES == n % EDGE + jnp.where(n < LANES, edge, inner))
        )
    rows_z[...] = z_stencil()
    for fetch in fetches:
        fetch.wait()
    tables = Tables(col, cnt, nbr, rate)
    level[...] = coarse_ref[...].astype(F32)
    rates = tables.rates(ROWS, EDGE)
    coarse_rates = tables.rates(CROWS, HALF)
    stencil, double, pairs = tables.row_stencil(), copies(ROWS, 2), pair_rows()
    messages = []
    for top in (True, False):
        tile = high_ref if top else low_ref
        both = mm(jnp.concatenate([tile[s] for s in range(SLOTS)], axis=1), packs[int(top)])
        row = both[:, :LANES].astype(BF16)
        near = level[pl.ds(HALF - 1 if top else 0, CROWS, stride=HALF), :]
        following = level[pl.ds(HALF - 2 if top else 1, CROWS, stride=HALF), :]
        near_fine = mm(double, near.astype(BF16)).astype(BF16)
        around = mm(jnp.concatenate([row, near_fine], axis=1), stencil) + mm(rows_z[...], row) + both[:, LANES:]
        half = (both[:, :LANES] + 2.0 * rates * around).astype(BF16)
        place = tables.to_coarse(3 if top else 2)
        sums = mm(pairs, jnp.concatenate([row, half], axis=1)).astype(BF16)
        cover = jnp.minimum(mm(jnp.ones((HALF, LANES), BF16), place), 1.0)
        flux = 0.25 * coarse_rates * mm(sums, jnp.concatenate([place, place], axis=0))
        flux = flux - coarse_rates * near * cover[:1]
        messages.append(
            (
                (Y_NEAR, near.astype(BF16)),
                (Y_NEXT, following.astype(BF16)),
                (Y_ROW, row),
                (Y_HALF, half),
                (Y_FLUX, flux.astype(BF16)),
                (Y_COVER, cover.astype(BF16)),
            )
        )
    store_by_parity("fine", near_ref, far_ref, *messages)


def sort_arrivals(axis, near_ref, far_ref, arrived):
    even = lax.axis_index(axis) % 2 == 0

    @pl.when(even)
    def _():
        arrived[0] = far_ref[...]
        arrived[1] = near_ref[...]

    @pl.when(jnp.logical_not(even))
    def _():
        arrived[0] = near_ref[...]
        arrived[1] = far_ref[...]


TALL = 8 * EDGE
PLANES = 16


def plane_rows(per, scale_inner):
    rows = COMPS * per
    out, src = iota((PLANES, rows), 0), iota((PLANES, rows), 1)
    c, last = out % 8, out >= 8
    edge = src == jnp.where(last, c * per + per - 1, c * per)
    real = c < COMPS
    if not scale_inner:
        return ones_at(edge & real)
    inner = src == jnp.where(last, c * per + per - 2, c * per + 1)
    return jnp.where(edge & real, -6.0, jnp.where(inner & real, 1.0, 0.0)).astype(BF16)


def store_by_parity(axis, near_ref, far_ref, up, down):
    even = lax.axis_index(axis) % 2 == 0

    @pl.when(even)
    def _():
        for at, value in up:
            near_ref[at : at + value.shape[0], :] = value
        for at, value in down:
            far_ref[at : at + value.shape[0], :] = value

    @pl.when(jnp.logical_not(even))
    def _():
        for at, value in down:
            near_ref[at : at + value.shape[0], :] = value
        for at, value in up:
            far_ref[at : at + value.shape[0], :] = value


def coarse_planes(coarse_ref, zs):
    return jnp.concatenate(
        [coarse_ref[pl.ds((c * HALF + z) * HALF, HALF), :] for z in zs for c in range(COMPS)], axis=0
    )


def interior_kernel(
    col, cnt, nbr, rate, fine_ref, coarse_ref, weights, side_sum, half_ref, edges_ref, planes_ref, flux_ref, place_ref,
    flux, summed, split,
):
    tables = Tables(col, cnt, nbr, rate)
    m, n = iota((CELLS, LANES), 0), iota((CELLS, LANES), 1)
    picked = jnp.where(m % HALF == n % HALF, mm(coarse_ref[...], tables.side_pick()), 0.0).astype(BF16)
    sides = [part.astype(BF16) for part in slot_sides(mm(side_sum[...], picked))]
    fields = [fine_ref[s] for s in range(SLOTS)]
    partners = partner_columns(lambda t: fine_ref[t], tables, ROWS)
    rows_z = z_stencil()
    rates = tables.rates(ROWS, EDGE)
    rates2 = 2.0 * jnp.concatenate([rates, rates], axis=1)
    place_ref[...] = tables.pool_spread(0)
    summed[...] = jnp.zeros(summed.shape, F32)
    planes_ref[...] = jnp.zeros(planes_ref.shape, F32)
    for q in range(4):
        lanes = slice(QUAD * q, QUAD * (q + 1))
        terms = plane_terms(fields, partners, sides, q, weights)
        for s in range(SLOTS):
            field = fields[s][:, lanes]
            start = field.astype(F32)
            value = start + rates2 * (terms[ROWS * s : ROWS * (s + 1)] + mm(rows_z, field))
            half_ref[s, :, lanes] = value.astype(BF16)
            if q == 0:
                edges_ref[s, :, :LANES] = value[:, :LANES]
            if q == 3:
                edges_ref[s, :, LANES:] = value[:, LANES:]
            both = value + start
            for h in range(2):
                part = slice(LANES * h, LANES * (h + 1))
                at = slice(QUAD * q + LANES * h, QUAD * q + LANES * (h + 1))
                split[2 * h, :ROWS, :] = value[:, part]
                split[2 * h + 1, :ROWS, :] = both[:, part]
                for p in range(2):
                    first = (EDGE - 1) * p
                    planes_ref[s, 8 * p : 8 * p + COMPS, at] = split[2 * h, pl.ds(first, COMPS, stride=EDGE), :]
                    row = PLANES * (2 * q + h) + 8 * p
                    summed[row : row + COMPS, LANES * s : LANES * (s + 1)] = (
                        split[2 * h + 1, pl.ds(first, COMPS, stride=EDGE), :]
                    )
    cells = mm(summed[...].astype(BF16), place_ref[...])
    for k in range(8):
        part = cells[PLANES * k : PLANES * (k + 1)]
        flux[pl.ds(2 * k, PLANES, stride=HALF), :] = part[:, :LANES]
        flux[pl.ds(2 * k + 1, PLANES, stride=HALF), :] = part[:, LANES:]
    cover = jnp.minimum(mm(jnp.ones((HALF, LANES), BF16), tables.to_coarse(None)), 1.0)
    coarse_rates = tables.rates(CROWS, HALF)
    for p in range(2):
        near = coarse_planes(coarse_ref, ((HALF - 1) * p,)).astype(F32)
        total = 0.25 * coarse_rates * flux[8 * HALF * p : 8 * HALF * p + CROWS, :]
        flux_ref[CROWS * p : CROWS * (p + 1), :] = total - coarse_rates * near * cover[:1]


def z_message_kernel(col, cnt, nbr, rate, coarse_ref, flux_in, y_near, y_far, near_ref, far_ref, arrived, flux):
    tables = Tables(col, cnt, nbr, rate)
    sort_arrivals("fine", y_near, y_far, arrived)
    flux[: 2 * CROWS, :] = flux_in[...]
    fine_pick, coarse_pick = plane_rows(EDGE, False), plane_rows(HALF, False)
    place = tables.to_coarse(None)
    rates = chain(iota((PLANES, LANES), 0) % 8, tables.rate + [jnp.zeros((), F32)] * 3)
    corners = []
    for k, face in ((0, 2), (1, 3)):
        row = mm(fine_pick, arrived[k, Y_ROW : Y_ROW + ROWS, :]).astype(BF16)
        corner = mm(coarse_pick, arrived[k, Y_NEAR : Y_NEAR + CROWS, :]).astype(BF16)
        corners.append(corner)
        ghost = mm(
            jnp.concatenate([row, corner], axis=1),
            jnp.concatenate([tables.linked_lanes(face), tables.from_coarse(face, True)], axis=0),
        )
        gain = (0.5 * rates * rates) * mm(ghost.astype(BF16), place)
        for p in range(2):
            at = pl.ds(CROWS * p + (HALF - 1) * k, COMPS, stride=HALF)
            flux[at, :] = flux[at, :] + gain[8 * p : 8 * p + COMPS]
    cover = jnp.minimum(mm(jnp.ones((HALF, LANES), BF16), place), 1.0).astype(BF16)
    messages = []
    for top in (True, False):
        near, following = (HALF - 1, HALF - 2) if top else (0, 1)
        messages.append(
            (
                (Z_NEAR, coarse_planes(coarse_ref, (near,))),
                (Z_NEXT, coarse_planes(coarse_ref, (following,))),
                (Z_FLUX, flux[CROWS * top : CROWS * (top + 1), :].astype(BF16)),
                (Z_LOW, corners[0]),
                (Z_HIGH, corners[1]),
                (Z_COVER, cover),
            )
        )
    store_by_parity("own", near_ref, far_ref, *messages)


SPAN = 32
DEEP = HALF + 2


def at_cell(c, z, y):
    return (c * DEEP + z + 1) * SPAN + 8 + y


def mixed(centre, total, r):
    total = total + pltpu.roll(centre, 1, 1) + pltpu.roll(centre, LANES - 1, 1)
    return centre + (0.5 * r) * (total - 6.0 * centre)


def own_mean(old, mean, tables, zs):
    for c in range(COMPS):
        for z in zs:
            total = (
                old[pl.ds(at_cell(c, z, -1), HALF), :]
                + old[pl.ds(at_cell(c, z, 1), HALF), :]
                + old[pl.ds(at_cell(c, z - 1, 0), HALF), :]
                + old[pl.ds(at_cell(c, z + 1, 0), HALF), :]
            )
            mean[pl.ds(at_cell(c, z, 0), HALF), :] = mixed(
                old[pl.ds(at_cell(c, z, 0), HALF), :], total, tables.rate[c]
            )


def strip_mean(old, mean, y_arr, tables):
    for c in range(COMPS):
        for k, y, inside in ((0, -1, 0), (1, HALF, HALF - 1)):
            at = Y_NEXT + c * HALF
            total = (
                y_arr[k, at : at + HALF, :].astype(F32)
                + old[pl.ds(at_cell(c, 0, inside), HALF, stride=SPAN), :]
                + old[pl.ds(at_cell(c, -1, y), HALF, stride=SPAN), :]
                + old[pl.ds(at_cell(c, 1, y), HALF, stride=SPAN), :]
            )
            mean[pl.ds(at_cell(c, 0, y), HALF, stride=SPAN), :] = mixed(
                old[pl.ds(at_cell(c, 0, y), HALF, stride=SPAN), :], total, tables.rate[c]
            )


def fill_old(old, coarse_ref, y_arr, zs):
    for c in range(COMPS):
        for z in zs:
            old[pl.ds(at_cell(c, z, 0), HALF), :] = coarse_ref[pl.ds((c * HALF + z) * HALF, HALF), :].astype(F32)
        for k, y in ((0, -1), (1, HALF)):
            at = Y_NEAR + c * HALF
            old[pl.ds(at_cell(c, 0, y), HALF, stride=SPAN), :] = y_arr[k, at : at + HALF, :].astype(F32)


def neighbour_rows(fine_ref, k):
    m, n = iota((SLOTS * LANES, LANES), 0), iota((SLOTS * LANES, LANES), 1)
    edge = LANES - EDGE if k else 0
    pack = ones_at((m // LANES == n // EDGE) & (m % LANES == n % EDGE + edge))
    tile = PLANE - LANES if k else 0
    return mm(jnp.concatenate([fine_ref[s, :, tile : tile + LANES] for s in range(SLOTS)], axis=1), pack)


class CoarseLanes:
    def __init__(self, tables, y_arr):
        x = iota((HALF, LANES), 1)
        covered, left, right = x < 0, x < 0, x < 0
        for s in range(SLOTS):
            x0, used = tables.start[s], tables.used[s] > 0
            covered = covered | ((x >= x0) & (x < x0 + HALF) & used)
            left = left | ((x == (x0 - 1) % LANES) & used & (tables.near[0][s] < 0))
            right = right | ((x == (x0 + HALF) % LANES) & used & (tables.near[1][s] < 0))
        self.covered = covered
        self.left, self.right = jnp.where(left, 1.0, 0.0), jnp.where(right, 1.0, 0.0)
        self.sides = self.left + self.right
        self.beside = [y_arr[k, Y_COVER : Y_COVER + HALF, :].astype(F32)[:1] for k in (0, 1)]

    def update(self, r, level0, level1, average, change):
        low, high = pltpu.roll(level0, LANES - 1, 1), pltpu.roll(level0, 1, 1)
        change = change - r * (self.sides * level1 + self.left * low + self.right * high)
        return jnp.where(self.covered, 0.125 * average, 2.0 * level1 - level0 + change).astype(BF16)

    def beyond_y(self, k, r, level0, level1, flux, corner):
        gain = (2.0 * r * r) * level0 - r * level1
        if corner is not None:
            gain = gain + (r * r) * corner
        return flux + self.beside[k] * gain


def early_kernel(*refs):
    ins, outs, scratch = refs[:14], refs[14:19], refs[19:]

    @pl.when(lax.axis_index("own") == 0)
    def _():
        middle_fine(*ins, *outs, *scratch)


def late_kernel(*refs):
    ins, done, coarse_out, faces_ref, outs, scratch = refs[:14], refs[14:19], refs[19], refs[20], refs[21:25], refs[25:]
    pairs, strips, y_arr, old, mean, split, average, outside = scratch
    is_early = lax.axis_index("own") == 0

    @pl.when(jnp.logical_not(is_early))
    def _():
        middle_fine(*ins, *outs, pairs, strips, y_arr, old, mean, split)

    @pl.when(is_early)
    def _():
        for source, target in zip(done, (*outs, pairs)):
            target[...] = source[...]
        levels(Tables(*ins[:4]), ins[5], ins[6], ins[7], y_arr, old, mean)

    middle_coarse(Tables(*ins[:4]), ins[13], pairs, y_arr, old, mean, average, outside, coarse_out, faces_ref)


def levels(tables, coarse_ref, y_near, y_far, y_arr, old, mean):
    sort_arrivals("fine", y_near, y_far, y_arr)
    fill_old(old, coarse_ref, y_arr, range(HALF))
    for c in range(COMPS):
        for z in (-1, HALF):
            old[pl.ds(at_cell(c, z, 0) - 8, SPAN), :] = jnp.zeros((SPAN, LANES), F32)
    own_mean(old, mean, tables, range(HALF))
    strip_mean(old, mean, y_arr, tables)


def middle_fine(
    col, cnt, nbr, rate, fine_ref, coarse_ref, y_near, y_far, half_in, edges_ref, planes_in, weights, side_sum, place_ref,
    fine_out, rows_ref, planes_ref, theirs_ref, pairs, strips, y_arr, old, mean, split,
):
    tables = Tables(col, cnt, nbr, rate)
    levels(tables, coarse_ref, y_near, y_far, y_arr, old, mean)
    rates = tables.rates(ROWS, EDGE)
    rates2 = 2.0 * jnp.concatenate([rates, rates], axis=1)
    double, rows_z = copies(ROWS, 2), z_stencil()
    cells = jnp.concatenate(
        [mean[pl.ds(at_cell(c, z, 0), HALF), :] for c in range(COMPS) for z in range(HALF)], axis=0
    ).astype(BF16)
    m, n = iota((CELLS, LANES), 0), iota((CELLS, LANES), 1)
    picked = jnp.where(m % HALF == n % HALF, mm(cells, tables.side_pick()), 0.0).astype(BF16)
    sides = [part.astype(BF16) for part in slot_sides(mm(side_sum[...], picked))]

    def level_row(level, y):
        rows = [level[pl.ds(at_cell(c, 0, y), HALF, stride=SPAN), :] for c in range(COMPS)]
        return mm(double, jnp.concatenate(rows, axis=0).astype(BF16)).astype(BF16)

    planes_ref[...] = planes_in[...]

    def half(t):
        return jnp.concatenate([strips[t, :, :LANES], half_in[t, :, LANES : PLANE - LANES], strips[t, :, LANES:]], axis=1)

    second = []
    plane_rates = chain(iota((PLANES, LANES), 0) % 8, tables.rate + [jnp.zeros((), F32)] * 3)
    for k, y in ((0, -1), (1, HALF)):
        linked, opened = tables.linked_lanes(2 + k), tables.from_coarse(2 + k, True)
        row = y_arr[k, Y_ROW : Y_ROW + ROWS, :]
        ghost = mm(jnp.concatenate([row, level_row(old, y)], axis=1), jnp.concatenate([linked, opened], axis=0))
        plane_ghost = mm(plane_rows(EDGE, False), ghost.astype(BF16))
        tile = slice(PLANE - LANES, PLANE) if k else slice(0, LANES)
        part = slice(LANES * k, LANES * (k + 1))
        for s in range(SLOTS):
            add = edge_lanes(ghost, s, bool(k))[:, part]
            strips[s, :, part] = (edges_ref[s, :, part] + 2.0 * rates * add).astype(BF16)
            add = edge_lanes(plane_ghost, s, bool(k))[:, part]
            planes_ref[s, :, tile] = planes_ref[s, :, tile] + 2.0 * plane_rates * add
        theirs = mm(y_arr[k, Y_HALF : Y_HALF + ROWS, :], linked) + 2.0 * rates * neighbour_rows(fine_ref, k)
        theirs_ref[k, :ROWS, :] = theirs
        theirs = theirs.astype(BF16).astype(F32)
        is_linked = chain(iota((ROWS, LANES), 1) // EDGE, tables.near[2 + k]) >= 0
        second.append(jnp.where(is_linked, theirs, mm(level_row(mean, y), opened)))

    rows_ref[...] = jnp.zeros(rows_ref.shape, F32)
    fields = [half(s) for s in range(SLOTS)]
    partners = partner_columns(half, tables, ROWS)
    for q in range(4):
        lanes = slice(QUAD * q, QUAD * (q + 1))
        terms = plane_terms(fields, partners, sides, q, weights)
        for s in range(SLOTS):
            field = fields[s][:, lanes]
            around = terms[ROWS * s : ROWS * (s + 1)] + mm(rows_z, field)
            if q == 0:
                around = around + edge_lanes(second[0], s, False)
            if q == 3:
                around = around + edge_lanes(second[1], s, True)
            start = field.astype(F32)
            for h in range(2):
                split[h, :ROWS, :] = start[:, LANES * h : LANES * (h + 1)]
                split[h, ROWS : 2 * ROWS, :] = (
                    split[h, :ROWS, :] + fine_ref[s, :, QUAD * q + LANES * h : QUAD * q + LANES * (h + 1)].astype(F32)
                )
                pairs[0, 2 * q + h, :, LANES * s : LANES * (s + 1)] = (
                    split[h, pl.ds(ROWS, CROWS, stride=2), :] + split[h, pl.ds(ROWS + 1, CROWS, stride=2), :]
                ).astype(BF16)
                at = slice(QUAD * q + LANES * h, QUAD * q + LANES * (h + 1))
                for w, first in enumerate((1, 2, EDGE - 3, EDGE - 2)):
                    rows_ref[s, 8 * w : 8 * w + COMPS, at] = split[h, pl.ds(first, COMPS, stride=EDGE), :]
            value = jnp.where(tables.used[s] > 0, start + rates2 * around, 0.0).astype(BF16)
            fine_out[s, :, lanes] = value
            value = value.astype(F32)
            for h in range(2):
                split[h, 2 * ROWS : 3 * ROWS, :] = value[:, LANES * h : LANES * (h + 1)]
                pairs[1, 2 * q + h, :, LANES * s : LANES * (s + 1)] = (
                    split[h, pl.ds(2 * ROWS, CROWS, stride=2), :] + split[h, pl.ds(2 * ROWS + 1, CROWS, stride=2), :]
                ).astype(BF16)


def middle_coarse(tables, place_ref, pairs, y_arr, old, mean, average, outside, coarse_out, faces_ref):
    faces = mm(pairs[0].reshape(8 * CROWS, SLOTS * LANES), tables.pool_spread(1))
    cells = mm(pairs[1].reshape(8 * CROWS, SLOTS * LANES), place_ref[...])
    coarse_rates = tables.rates(CROWS, HALF)
    scale = 0.25 * coarse_rates
    for j in range(2):
        lanes = slice(LANES * j, LANES * (j + 1))
        for k in range(8):
            at = pl.ds(2 * k + j, CROWS, stride=HALF)
            outside[at, :] = scale * faces[CROWS * k : CROWS * (k + 1), lanes]
            average[at, :] = cells[CROWS * k : CROWS * (k + 1), lanes]
    for c in range(COMPS):
        for p in range(2):
            at = CROWS * p + HALF * c
            faces_ref[at : at + HALF, :] = outside[pl.ds((c * HALF + (HALF - 1) * p) * HALF, HALF), :]

    masks = CoarseLanes(tables, y_arr)

    def strip(level, y):
        return jnp.concatenate([level[pl.ds(at_cell(c, 0, y), HALF, stride=SPAN), :] for c in range(COMPS)], axis=0)

    for k, y in ((0, 0), (1, HALF - 1)):
        at = pl.ds(y, CROWS, stride=HALF)
        flux = y_arr[k, Y_FLUX : Y_FLUX + CROWS, :].astype(F32)
        outside[at, :] = outside[at, :] + masks.beyond_y(k, coarse_rates, strip(old, y), strip(mean, y), flux, None)
    for c in range(COMPS):
        for z in range(HALF):
            line = pl.ds((c * HALF + z) * HALF, HALF)
            if z in (0, HALF - 1):
                coarse_out[line, :] = jnp.zeros((HALF, LANES), BF16)
                continue
            coarse_out[line, :] = masks.update(
                tables.rate[c], old[pl.ds(at_cell(c, z, 0), HALF), :], mean[pl.ds(at_cell(c, z, 0), HALF), :],
                average[line, :], outside[line, :],
            )


NEAR = 32


def last_kernel(
    col, cnt, nbr, rate, coarse_ref, y_near, y_far, z_near, z_far, weights, place_ref,
    coarse_in, fine_in, rows_ref, planes_ref, theirs_ref, faces_ref,
    coarse_out, fine_hbm, y_arr, z_arr, old, mean, near, split, following, spread, ghost, level_rows, put, fine_out, sems,
):
    tables = Tables(col, cnt, nbr, rate)
    sort_arrivals("fine", y_near, y_far, y_arr)
    sort_arrivals("own", z_near, z_far, z_arr)
    fill_old(old, coarse_ref, y_arr, (0, 1, HALF - 2, HALF - 1))
    for k in (0, 1):
        following[k, :CROWS, :] = y_arr[k, Y_NEXT : Y_NEXT + CROWS, :].astype(F32)
    for c in range(COMPS):
        for k, z in ((0, -1), (1, HALF)):
            at = Z_NEAR + c * HALF
            old[pl.ds(at_cell(c, z, 0), HALF), :] = z_arr[k, at : at + HALF, :].astype(F32)
    by_comp = DEEP * SPAN
    for k, z in ((0, -1), (1, HALF)):
        first = 0 if k else 8
        low = z_arr[k, Z_LOW : Z_LOW + HALF, :].astype(F32)
        high = z_arr[k, Z_HIGH : Z_HIGH + HALF, :].astype(F32)
        old[pl.ds(at_cell(0, z, -1), COMPS, stride=by_comp), :] = low[first : first + COMPS]
        old[pl.ds(at_cell(0, z, HALF), COMPS, stride=by_comp), :] = high[first : first + COMPS]
    own_mean(old, mean, tables, (0, HALF - 1))
    comp_rates = chain(iota((COMPS, LANES), 0), tables.rate)
    level_rows[...] = jnp.zeros(level_rows.shape, F32)
    for k, y, inside in ((0, -1, 0), (1, HALF, HALF - 1)):
        for p, z in ((0, 0), (1, HALF - 1)):
            total = (
                following[k, pl.ds(z, COMPS, stride=HALF), :]
                + old[pl.ds(at_cell(0, z, inside), COMPS, stride=by_comp), :]
                + old[pl.ds(at_cell(0, z - 1, y), COMPS, stride=by_comp), :]
                + old[pl.ds(at_cell(0, z + 1, y), COMPS, stride=by_comp), :]
            )
            value = mixed(old[pl.ds(at_cell(0, z, y), COMPS, stride=by_comp), :], total, comp_rates)
            for w in (2 * p, 2 * p + 1):
                level_rows[k, 8 * w : 8 * w + COMPS, :] = value
    for c in range(COMPS):
        for k, z, inside in ((0, -1, 0), (1, HALF, HALF - 1)):
            at = Z_NEXT + c * HALF
            total = (
                z_arr[k, at : at + HALF, :].astype(F32)
                + old[pl.ds(at_cell(c, inside, 0), HALF), :]
                + old[pl.ds(at_cell(c, z, -1), HALF), :]
                + old[pl.ds(at_cell(c, z, 1), HALF), :]
            )
            mean[pl.ds(at_cell(c, z, 0), HALF), :] = mixed(
                old[pl.ds(at_cell(c, z, 0), HALF), :], total, tables.rate[c]
            )

    window = tables.from_coarse(None, False)
    n = iota((2 * CROWS, LANES), 1)

    def planes_of(level, zs):
        return jnp.concatenate([level[pl.ds(at_cell(c, z, 0), HALF), :] for z in zs for c in range(COMPS)], axis=0)

    first_y = iota((COMPS, LANES), 1) < 2 * EDGE

    def ghost_rows(level, i):
        planes = mm(planes_of(level, (-1, HALF)).astype(BF16), window)
        for s in range(SLOTS):
            part = jnp.where(n // EDGE == s, planes, 0.0)
            part = part + pltpu.roll(part, EDGE, 1)
            spread[s, : 2 * CROWS, :] = part + pltpu.roll(part, 2 * EDGE, 1)
            for k in range(8):
                for p in range(2):
                    even = spread[s, pl.ds(CROWS * p + 2 * k, COMPS, stride=HALF), :]
                    odd = spread[s, pl.ds(CROWS * p + 2 * k + 1, COMPS, stride=HALF), :]
                    ghost[i, s, 8 * p : 8 * p + COMPS, LANES * k : LANES * (k + 1)] = jnp.where(first_y, even, odd)

    ghost[...] = jnp.zeros(ghost.shape, F32)
    ghost_rows(old, 0)
    ghost_rows(mean, 1)
    rates = chain(iota((NEAR, LANES), 0) % 8, tables.rate + [jnp.zeros((), F32)] * 3)
    rates2 = 2.0 * jnp.concatenate([rates, rates], axis=1)
    wide = 2.0 * chain(iota((2 * 8, PLANE), 0) % 8, tables.rate + [jnp.zeros((), F32)] * 3)

    along = []
    for s in range(SLOTS):
        ends = (planes_ref[s] + wide * ghost[0, s]).astype(BF16).astype(F32)
        one, two, next_last, last = (rows_ref[s, 8 * w : 8 * (w + 1), :] for w in range(4))
        near[s] = jnp.concatenate([ends[:8], one, last, ends[8:]], axis=0).astype(BF16)
        along.append(
            jnp.concatenate(
                [
                    one - 6.0 * ends[:8] + ghost[1, s, :8],
                    ends[:8] + two - 6.0 * one,
                    ends[8:] + next_last - 6.0 * last,
                    last - 6.0 * ends[8:] + ghost[1, s, 8:],
                ],
                axis=0,
            )
        )

    m = iota((2 * CROWS, LANES), 0)
    picked = jnp.where(
        m % HALF == n % HALF, mm(planes_of(mean, (0, HALF - 1)).astype(BF16), tables.side_pick()), 0.0
    ).astype(BF16)
    out, src = iota((NEAR, 2 * CROWS), 0), iota((NEAR, 2 * CROWS), 1)
    side_sum = ones_at((out % 8 == src % CROWS // HALF) & (out % 8 < COMPS) & (out // 16 == src // CROWS))
    sides = [part.astype(BF16) for part in slot_sides(mm(side_sum, picked))]
    ghosts = []
    zero = jnp.zeros((8, LANES), F32)
    for k in (0, 1):
        at = Z_HIGH if k else Z_LOW
        corner = jnp.concatenate([z_arr[0, at : at + PLANES, :], z_arr[1, at : at + PLANES, :]], axis=0)
        corner = mm(corner, window)
        for w, first in enumerate((0, 1, EDGE - 2, EDGE - 1)):
            level_rows[2, 8 * w : 8 * w + COMPS, :] = theirs_ref[k, pl.ds(first, COMPS, stride=EDGE), :]
        theirs = level_rows[2] + 2.0 * rates * jnp.concatenate([corner[8:16], zero, zero, corner[16:24]], axis=0)
        theirs = theirs.astype(BF16).astype(F32)
        is_linked = chain(iota((NEAR, LANES), 1) // EDGE, tables.near[2 + k]) >= 0
        level = mm(level_rows[k].astype(BF16), tables.from_coarse(2 + k, True))
        ghosts.append(jnp.where(is_linked, theirs, level))
    fields = [near[s] for s in range(SLOTS)]
    partners = partner_columns(lambda t: near[t], tables, NEAR)
    fresh = []
    for q in range(4):
        lanes = slice(QUAD * q, QUAD * (q + 1))
        terms = plane_terms(fields, partners, sides, q, weights)
        for s in range(SLOTS):
            field = fields[s][:, lanes]
            around = terms[NEAR * s : NEAR * (s + 1)] + along[s][:, lanes]
            if q == 0:
                around = around + edge_lanes(ghosts[0], s, False)
            if q == 3:
                around = around + edge_lanes(ghosts[1], s, True)
            value = jnp.where(tables.used[s] > 0, field.astype(F32) + rates2 * around, 0.0).astype(BF16)
            fresh.append(value)
            value = value.astype(F32)
            for h in range(2):
                for w, first in enumerate((0, 1, EDGE - 2, EDGE - 1)):
                    put[s, 2 * q + h, pl.ds(first, COMPS, stride=EDGE), :] = (
                        value[8 * w : 8 * w + COMPS, LANES * h : LANES * (h + 1)]
                    )
    a = iota((ROWS, LANES), 0) % EDGE
    replaced = (a < 2) | (a >= EDGE - 2)
    sends = []
    for s in range(SLOTS):
        for k in range(8):
            lanes = slice(LANES * k, LANES * (k + 1))
            fine_out[s, :, lanes] = jnp.where(replaced, put[s, k, :ROWS, :], fine_in[s, :, lanes].astype(F32)).astype(BF16)
        sends.append(pltpu.make_async_copy(fine_out.at[s], fine_hbm.at[s], sems.at[s]))
        sends[s].start()

    tall = jnp.concatenate(
        [
            jnp.concatenate([fresh[SLOTS * q + s][:, LANES * h : LANES * (h + 1)] for s in range(SLOTS)], axis=1)
            for q in range(4)
            for h in range(2)
        ],
        axis=0,
    )
    cells = mm(tall, place_ref[...])
    for k in range(8):
        part = cells[NEAR * k : NEAR * (k + 1)]
        for j in range(2):
            lane = slice(LANES * j, LANES * (j + 1))
            for p in range(2):
                pair = part[16 * p : 16 * p + 8, lane] + part[16 * p + 8 : 16 * p + 16, lane]
                split[pl.ds(8 * HALF * p + 2 * k + j, 8, stride=HALF), :] = pair

    coarse_out[...] = coarse_in[...]
    masks = CoarseLanes(tables, y_arr)
    row = iota((HALF, LANES), 0)
    for c in range(COMPS):
        r = tables.rate[c]
        y_flux = [y_arr[k, Y_FLUX + c * HALF : Y_FLUX + (c + 1) * HALF, :].astype(F32) for k in (0, 1)]
        for p, z in ((0, 0), (1, HALF - 1)):
            beyond = -1 if z == 0 else HALF
            level0, level1 = old[pl.ds(at_cell(c, z, 0), HALF), :], mean[pl.ds(at_cell(c, z, 0), HALF), :]
            halo = old[pl.ds(at_cell(c, beyond, 0), HALF), :]
            halo = masks.left * pltpu.roll(halo, LANES - 1, 1) + masks.right * pltpu.roll(halo, 1, 1)
            at = CROWS * p + HALF * c
            change = faces_ref[at : at + HALF, :] + (r * r) * halo
            for k, y in ((0, 0), (1, HALF - 1)):
                corner = old[pl.ds(at_cell(c, beyond, HALF if k else -1), 1), :]
                extra = masks.beyond_y(k, r, level0[y : y + 1], level1[y : y + 1], y_flux[k][z : z + 1], corner)
                change = change + jnp.where(row == y, extra, 0.0)
            flux = z_arr[p, Z_FLUX + c * HALF : Z_FLUX + (c + 1) * HALF, :].astype(F32)
            ahead = z_arr[p, Z_COVER : Z_COVER + HALF, :].astype(F32)
            change = change + flux + ahead * ((2.0 * r * r) * level0 - r * level1)
            coarse_out[pl.ds((c * HALF + z) * HALF, HALF), :] = masks.update(
                r, level0, level1, split[pl.ds(8 * HALF * p + c * HALF, HALF), :], change
            )
    for send in sends:
        send.wait()


SCALARS = [pl.BlockSpec(memory_space=pltpu.SMEM)] * 4
PARAMS = pltpu.CompilerParams(vmem_limit_bytes=32 * 1024 * 1024)
FETCH_PARAMS = pltpu.CompilerParams(vmem_limit_bytes=60 * 1024 * 1024)


def whole():
    return pl.BlockSpec(memory_space=pltpu.VMEM)


def local(coarse_cells, fine_cells, diffusivity, patch_column, patch_count, neighbor_slot):
    fine = fine_cells.reshape(SLOTS, ROWS, PLANE)
    coarse = coarse_cells.reshape(CELLS, LANES)
    tables = (patch_column, patch_count, neighbor_slot, diffusivity)
    n_own, n_fine = lax.axis_size("own"), lax.axis_size("fine")

    def swap(value, axis, count, far):
        shift = 1 if far else 0
        pairs = []
        for i in range(count):
            partner = ((i - shift) ^ 1) + shift
            pairs.append((i, partner % count))
        return lax.ppermute(value, axis, pairs)

    y_shape = jax.ShapeDtypeStruct((Y_ROWS, LANES), BF16)
    field_shape = jax.ShapeDtypeStruct((SLOTS, ROWS, PLANE), BF16)
    cells_shape = jax.ShapeDtypeStruct((CELLS, LANES), BF16)
    y_near, y_far = pl.pallas_call(
        y_message_kernel,
        in_specs=[pl.BlockSpec(memory_space=pl.ANY)] * 6,
        out_specs=[whole()] * 2,
        out_shape=[y_shape] * 2,
        scratch_shapes=[
            pltpu.SMEM((SLOTS,), jnp.int32),
            pltpu.SMEM((1,), jnp.int32),
            pltpu.SMEM((SLOTS, 4), jnp.int32),
            pltpu.SMEM((COMPS,), F32),
            pltpu.VMEM((SLOTS, ROWS, LANES), BF16),
            pltpu.VMEM((SLOTS, ROWS, LANES), BF16),
            pltpu.VMEM((CELLS, LANES), BF16),
            pltpu.VMEM((CELLS, LANES), F32),
            pltpu.VMEM((2, SLOTS * LANES, QUAD), BF16),
            pltpu.VMEM((ROWS, ROWS), BF16),
            pltpu.SemaphoreType.DMA((7,)),
        ],
        compiler_params=FETCH_PARAMS,
        name="y_messages",
    )(*tables, fine, coarse)
    y_near, y_far = swap(y_near, "fine", n_fine, False), swap(y_far, "fine", n_fine, True)

    planes_shape = jax.ShapeDtypeStruct((SLOTS, PLANES, PLANE), F32)
    level = pltpu.VMEM((COMPS * DEEP * SPAN, LANES), F32)
    weights, side_sum = jnp.asarray(plane_weights()), jnp.asarray(side_rows())
    half, edges, planes, flux, place = pl.pallas_call(
        interior_kernel,
        in_specs=SCALARS + [whole()] * 4,
        out_specs=[whole()] * 5,
        out_shape=[
            field_shape,
            jax.ShapeDtypeStruct((SLOTS, ROWS, QUAD), F32),
            planes_shape,
            jax.ShapeDtypeStruct((2 * CROWS, LANES), F32),
            jax.ShapeDtypeStruct((SLOTS * LANES, QUAD), BF16),
        ],
        scratch_shapes=[
            pltpu.VMEM((PLANES * HALF, LANES), F32),
            pltpu.VMEM((8 * PLANES, SLOTS * LANES), F32),
            pltpu.VMEM((4, TALL, LANES), F32),
        ],
        compiler_params=PARAMS,
        cost_estimate=pl.CostEstimate(flops=2_000_000_000, bytes_accessed=5_000_000, transcendentals=0),
        name="interior",
    )(*tables, fine, coarse, weights, side_sum)

    z_shape = jax.ShapeDtypeStruct((Z_ROWS, LANES), BF16)
    z_near, z_far = pl.pallas_call(
        z_message_kernel,
        in_specs=SCALARS + [whole()] * 4,
        out_specs=[whole()] * 2,
        out_shape=[z_shape] * 2,
        scratch_shapes=[pltpu.VMEM((2, Y_ROWS, LANES), BF16), pltpu.VMEM((TALL, LANES), F32)],
        compiler_params=PARAMS,
        name="z_messages",
    )(*tables, coarse, flux, y_near, y_far)
    fine_shapes = [
        field_shape,
        jax.ShapeDtypeStruct((SLOTS, 32, PLANE), F32),
        planes_shape,
        jax.ShapeDtypeStruct((2, TALL, LANES), F32),
    ]
    pairs_shape = (2, 8, CROWS, SLOTS * LANES)
    middle_args = (*tables, fine, coarse, y_near, y_far, half, edges, planes, weights, side_sum, place)
    scratch = [
        pltpu.VMEM((SLOTS, ROWS, QUAD), BF16),
        pltpu.VMEM((2, Y_ROWS, LANES), BF16),
        level,
        level,
        pltpu.VMEM((2, 3 * ROWS, LANES), F32),
    ]
    z_near = swap(z_near, "own", n_own, False)
    done = pl.pallas_call(
        early_kernel,
        in_specs=SCALARS + [whole()] * 10,
        out_specs=[whole()] * 5,
        out_shape=fine_shapes + [jax.ShapeDtypeStruct(pairs_shape, BF16)],
        scratch_shapes=scratch,
        compiler_params=PARAMS,
        cost_estimate=pl.CostEstimate(flops=3_000_000_000, bytes_accessed=8_000_000, transcendentals=0),
        name="early",
    )(*middle_args)
    z_far, done = lax.optimization_barrier((z_far, done))
    z_far = swap(z_far, "own", n_own, True)
    coarse_part, faces, *parts = pl.pallas_call(
        late_kernel,
        in_specs=SCALARS + [whole()] * 15,
        out_specs=[whole()] * 6,
        out_shape=[cells_shape, jax.ShapeDtypeStruct((2 * CROWS, LANES), F32)] + fine_shapes,
        scratch_shapes=[
            pltpu.VMEM(pairs_shape, BF16),
            *scratch,
            pltpu.VMEM((CELLS, LANES), F32),
            pltpu.VMEM((CELLS, LANES), F32),
        ],
        compiler_params=PARAMS,
        cost_estimate=pl.CostEstimate(flops=3_000_000_000, bytes_accessed=8_000_000, transcendentals=0),
        name="late",
    )(*middle_args, *done)
    parts = (coarse_part, *parts, faces)

    coarse_new, fine_new = pl.pallas_call(
        last_kernel,
        in_specs=SCALARS + [whole()] * 13,
        out_specs=[whole(), pl.BlockSpec(memory_space=pl.ANY)],
        out_shape=[cells_shape, field_shape],
        scratch_shapes=[
            pltpu.VMEM((2, Y_ROWS, LANES), BF16),
            pltpu.VMEM((2, Z_ROWS, LANES), BF16),
            pltpu.VMEM((8 * DEEP * SPAN, LANES), F32),
            level,
            pltpu.VMEM((SLOTS, 32, PLANE), BF16),
            pltpu.VMEM((PLANES * HALF, LANES), F32),
            pltpu.VMEM((2, 8 * HALF, LANES), F32),
            pltpu.VMEM((SLOTS, TALL, LANES), F32),
            pltpu.VMEM((2, SLOTS, PLANES, PLANE), F32),
            pltpu.VMEM((3, 32, LANES), F32),
            pltpu.VMEM((SLOTS, 8, TALL, LANES), F32),
            pltpu.VMEM((SLOTS, ROWS, PLANE), BF16),
            pltpu.SemaphoreType.DMA((SLOTS,)),
        ],
        compiler_params=PARAMS,
        name="last",
    )(*tables, coarse, y_near, y_far, z_near, z_far, weights, place, *parts)
    return coarse_new.reshape(coarse_cells.shape), fine_new.reshape(fine_cells.shape)


def solution(mesh):
    return jax.shard_map(
        local,
        mesh=mesh,
        in_specs=(
            P(None, "own", "fine", None),
            P(("own", "fine"), None, None, None),
            P(),
            P(("own", "fine")),
            P(("own", "fine")),
            P(("own", "fine"), None),
        ),
        out_specs=(P(None, "own", "fine", None), P(("own", "fine"), None, None, None)),
        check_vma=False,
    )
```
